32 devices in a mesh: mesh: 8 (over z, x), freq: 4 (over y, core).
Axes of the slice: x: 2, y: 2, z: 4, core: 2. Of those that a mesh axis runs over, the one named last changes fastest.
Arguments:
- spectra: float32 [36, 36, 4096], P('freq', None, 'mesh'), may hold values from 0.1 to 2
- coords: float32 [2, 4096], P(None, 'mesh'), may hold values from -5 to 5
- inv_area: float32 [4096], P('mesh'), may hold values from 0.3 to 1
- wind_vector: float32 [2, 4096], P(None, 'mesh'), may hold values from -6 to 6
- neighbours: int32 [8, 4096], P(None, 'mesh'), may hold values from 0 to 767, as said below
- send_nodes: int32 [64, 32], P('mesh'), may hold values from 0 to 511
- send_count: int32 [64], P('mesh'), may hold values from 1 to 32, as said below
Outputs:
- updated: float32 [36, 36, 4096], P('freq', None, 'mesh')
The draws below stay inside these ranges and needn't reach their ends.
Inputs may be any that keep to these rules, and one draw needn't show every extreme that they name: `neighbours`: an entry below 512 is a node of the same partition; an entry 512 + q * 32 + c names slot c of the list that partition q sends to this partition, with c below that list's count; slots past a node's degree name the node itself; some node uses all 8 slots. `send_count`: in every draw some partition receives exactly 32 nodes from every partition.
All inputs are finite; a program needn't handle non-finite values.
Results may differ from the reference program's by a relative error of at most 0.00002.
Values sent between devices are 32-bit elements; how exact they have to be, the bound alone decides.
A program may use at most 64 MiB of HBM per device.

```python
import math
import jax
import jax.numpy as jnp
from jax import lax

NF = 36
ND = 36
K = 8
REACH = 3
SWEEPS = 2
NP = 512
UP_SHIFT = 1
DOWN_SHIFT = 3
CAP = 32
NODES = 4096
PAIRS = 64


def counts_table(key):
    parts_count = NODES // NP
    key_fill = jax.random.fold_in(key, 11)
    key_full = jax.random.fold_in(key, 12)
    table = jax.random.randint(key_fill, (parts_count, parts_count), 1, CAP + 1)
    crowded = jax.random.randint(key_full, (), 0, parts_count)
    table = jnp.where(jnp.arange(parts_count)[None, :] == crowded, CAP, table)
    return table.reshape(-1).astype(jnp.int32)


def draw_send_count(key, part):
    return counts_table(key)


def draw_neighbours(key, part):
    parts_count = NODES // NP
    counts = counts_table(key)
    node_ids = jnp.arange(NODES, dtype=jnp.int32)
    owner = node_ids // NP
    own_local = node_ids % NP
    degree = jax.random.randint(jax.random.fold_in(key, 21), (NODES,), 3, K + 1)
    degree = jnp.where(node_ids == 0, K, degree)
    slot_ids = jnp.arange(K, dtype=jnp.int32)[:, None]
    kinds = jax.random.randint(jax.random.fold_in(key, 22), (K, NODES), 0, 4)
    local_pick = jax.random.randint(jax.random.fold_in(key, 23), (K, NODES), 0, NP)
    source = jax.random.randint(jax.random.fold_in(key, 24), (K, NODES), 0, parts_count)
    limit = counts[source * parts_count + owner[None, :]]
    place = jax.random.randint(jax.random.fold_in(key, 25), (K, NODES), 0, limit)
    ghost_entry = NP + source * CAP + place
    entry = jnp.where(kinds == 0, ghost_entry, local_pick)
    entry = jnp.where(slot_ids < degree[None, :], entry, own_local[None, :])
    return entry.astype(jnp.int32)


def set_ends(drawn, rng, low, top_value):
    index_at = [jax.random.randint(jax.random.fold_in(rng, axis), (), 0, length) for axis, length in enumerate(drawn.shape)]
    longest = drawn.shape.index(max(drawn.shape))
    beside = index_at[:longest] + [(index_at[longest] + 1) % drawn.shape[longest]] + index_at[longest + 1:]
    return drawn.at[tuple(index_at)].set(low).at[tuple(beside)].set(top_value)


def steps_of(stream_key, extent, split, smallest, high):
    loudness, own = 1.0, jax.random.fold_in(stream_key, 6)
    for position, blocks in split:
        heights = jnp.exp(jax.random.uniform(jax.random.fold_in(own, position), (blocks,), jnp.float32, smallest / len(split), high / len(split)))
        loudness = loudness * jnp.repeat(heights, extent[position] // blocks).reshape([-1 if axis == position else 1 for axis in range(len(extent))])
    return loudness


def centred(key, dims, width, most, pieces=(), held_as=jnp.bfloat16):
    array = jax.random.normal(key, dims, jnp.float32) * width
    if len(pieces) > 0:
        array = steps_of(key, dims, pieces, -0.22, 0.18) * array
    return jnp.clip(array, min=-most, max=most).astype(held_as)


def setup_inputs(seed: int = 0) -> dict:
    keys = jax.random.split(jax.random.key(seed), 8)
    spectra = jnp.clip(jnp.exp(math.log(2.0) - 2.9957323 * jax.random.uniform(keys[0], (NF, ND, NODES), jnp.float32) ** steps_of(keys[0], (NF, ND, NODES), ((0, 4), (2, 8)), -0.2, 0.2)), 0.1, 2.0)
    coords = centred(keys[1], (2, NODES), 1.0, 5.0, ((1, 8),), jnp.float32)
    inv_area = jnp.clip(jnp.exp(math.log(1.0) - 1.2039728 * jax.random.uniform(keys[2], (NODES,), jnp.float32) ** steps_of(keys[2], (NODES,), ((0, 8),), -0.2, 0.2)), 0.3, 1.0)
    wind_vector = centred(keys[3], (2, NODES), 1.5, 6.0, ((1, 8),), jnp.float32)
    neighbours = draw_neighbours(jax.random.fold_in(keys[7], 71), 0)
    send_nodes = set_ends(jax.random.randint(keys[5], (PAIRS, CAP), 0, NP), jax.random.fold_in(keys[5], 1), 0, NP - 1).astype(jnp.int32)
    send_count = draw_send_count(jax.random.fold_in(keys[7], 71), 0)
    return {"spectra": spectra, "coords": coords, "inv_area": inv_area, "wind_vector": wind_vector, "neighbours": neighbours, "send_nodes": send_nodes, "send_count": send_count}


time_step = 0.5
group_scale = 0.8
quad_coupling = 0.25
wind_growth = 0.1
freq_ratio = 1.1


def direction_tables():
    angles = (jnp.arange(ND, dtype=jnp.float32) + 0.5) * (2.0 * math.pi / ND)
    return jnp.cos(angles), jnp.sin(angles)


def source_terms(density, widened, ratios, wind_vector):
    band_count = density.shape[0]
    upper = lax.slice_in_dim(widened, REACH + REACH - 1, REACH + REACH - 1 + band_count, axis=0)
    lower = lax.slice_in_dim(widened, 0, band_count, axis=0)
    upper_left = jnp.roll(upper, -UP_SHIFT, axis=1)
    lower_left = jnp.roll(lower, DOWN_SHIFT, axis=1)
    upper_right = jnp.roll(upper, UP_SHIFT, axis=1)
    lower_right = jnp.roll(lower, -DOWN_SHIFT, axis=1)
    quad = quad_coupling * (density * density * (upper_left + lower_left + upper_right + lower_right)
                            - 2.0 * density * (upper_left * lower_left + upper_right * lower_right))
    cosine, sine = direction_tables()
    along = cosine[:, None] * wind_vector[0][None, :] + sine[:, None] * wind_vector[1][None, :]
    growth = wind_growth * jnp.maximum(along[None] * ratios[:, None, None] - 1.0, 0.0)
    return density + time_step * (quad + growth * density)


def inflow(ratios, inv_area, delta_x, delta_y):
    cosine, sine = direction_tables()
    speeds = group_scale / ratios
    facing = -(cosine[:, None] * delta_x[None, :] + sine[:, None] * delta_y[None, :])
    return (time_step * speeds)[:, None, None] * jnp.maximum(facing, 0.0)[None] * inv_area[None, None, :]


def reference(spectra, coords, inv_area, wind_vector, neighbours, send_nodes, send_count):
    parts_count = NODES // NP
    node_ids = jnp.arange(NODES, dtype=jnp.int32)
    owner = node_ids // NP
    ratios = jnp.power(freq_ratio, (jnp.arange(NF, dtype=jnp.int32) - NF // 2).astype(jnp.float32))
    widened = jnp.pad(spectra, ((REACH, REACH), (0, 0), (0, 0)))
    base = source_terms(spectra, widened, ratios, wind_vector)
    targets = []
    valids = []
    for slot_index in range(K):
        entry = neighbours[slot_index]
        is_local = entry < NP
        ghost = jnp.maximum(entry - NP, 0)
        source = ghost // CAP
        place = ghost % CAP
        pair = source * parts_count + owner
        remote = source * NP + send_nodes[pair, place]
        alive = place < send_count[pair]
        targets.append(jnp.where(is_local, owner * NP + entry, remote).astype(jnp.int32))
        valids.append(jnp.logical_or(is_local, alive).astype(jnp.float32))
    current = spectra
    for sweep_num in range(SWEEPS):
        total = base
        weight_sum = jnp.ones_like(spectra)
        for slot_index in range(K):
            target = targets[slot_index]
            valid = valids[slot_index]
            delta_x = coords[0][target] * valid - coords[0]
            delta_y = coords[1][target] * valid - coords[1]
            weights = inflow(ratios, inv_area, delta_x, delta_y)
            total = total + weights * (jnp.take(current, target, axis=2) * valid[None, None, :])
            weight_sum = weight_sum + weights
        current = total / weight_sum
    return current
```

```python
import functools
import math

import jax
import jax.numpy as jnp
from jax import lax
from jax.experimental import pallas as pl
from jax.experimental.pallas import tpu as pltpu
from jax.sharding import PartitionSpec as P

NF = 36
REACH = 3
UP_REACH = REACH - 1
UP_SHIFT = 1
DOWN_SHIFT = 3

time_step = 0.5
group_scale = 0.8
quad_coupling = 0.25
wind_growth = 0.1
freq_ratio = 1.1

MESH = pl.DeviceIdType.MESH
ROWS = 128
SPARE = 120
PER = 3
PITCH = 40


def split2(x):
    hi = x.astype(jnp.bfloat16)
    lo = (x - hi.astype(jnp.float32)).astype(jnp.bfloat16)
    return hi, lo


def roll_rows(x, shift):
    count = x.shape[0]
    cut = (-shift) % count
    return jnp.concatenate([x[cut:], x[:cut]], axis=0)


def kernel(
    n_mesh, n_freq, dirs, cap,
    spec_ref, coords_ref, inv_ref, wind_ref, nb_ref, send_ref, count_ref,
    out_ref,
    cur, lhs, picked, base, acc, weights, wsum, hot, hot_send, pay, recv, halo_lo, halo_hi,
    send_sem, recv_sem, halo_sem,
):
    band = spec_ref.shape[0]
    nodes = spec_ref.shape[2]
    slots = nb_ref.shape[0]
    ghosts = n_mesh * cap
    chunks = band // PER
    f32 = jnp.float32
    bf16 = jnp.bfloat16
    me = lax.axis_index("mesh")
    fi = lax.axis_index("freq")

    barrier = pltpu.get_barrier_semaphore()
    for off in range(1, n_mesh):
        pl.semaphore_signal(
            barrier, inc=1, device_id={"mesh": lax.rem(me + off, n_mesh)}, device_id_type=MESH
        )

    @pl.when(fi > 0)
    def _():
        pl.semaphore_signal(barrier, inc=1, device_id={"freq": fi - 1}, device_id_type=MESH)

    @pl.when(fi < n_freq - 1)
    def _():
        pl.semaphore_signal(barrier, inc=1, device_id={"freq": fi + 1}, device_id_type=MESH)

    cells = send_ref[...].astype(f32)
    lane_c = lax.broadcasted_iota(jnp.int32, (cap, ghosts), 1) % cap
    spread = (lane_c == lax.broadcasted_iota(jnp.int32, (cap, ghosts), 0)).astype(f32)
    wide = jnp.dot(cells, spread, precision=lax.Precision.HIGHEST, preferred_element_type=f32)
    owner_lane = lax.broadcasted_iota(jnp.int32, (n_mesh, ghosts), 1) // cap
    mine = owner_lane == lax.broadcasted_iota(jnp.int32, (n_mesh, ghosts), 0)
    send_row = jnp.sum(jnp.where(mine, wide, 0.0), axis=0, keepdims=True)
    send_row = (send_row + 0.5).astype(jnp.int32)
    lane = lax.broadcasted_iota(jnp.int32, (1, ghosts), 1)
    limit = jnp.zeros((1, ghosts), jnp.int32)
    for d in range(n_mesh):
        limit = jnp.where(lane // cap == d, count_ref[d], limit)
    send_row = jnp.where(lane % cap < limit, send_row, -1)
    hot_send[...] = (
        (lax.broadcasted_iota(jnp.int32, (nodes, ghosts), 0) == send_row).astype(f32).astype(bf16)
    )

    for c in range(chunks):
        cur[c] = jnp.zeros((ROWS, nodes), f32)
        for j in range(PER):
            cur[c, j * PITCH : j * PITCH + dirs, :] = spec_ref[c * PER + j]
    x_own = coords_ref[0:1, :]
    y_own = coords_ref[1:2, :]
    cur[0, SPARE : SPARE + 1, :] = x_own
    cur[0, SPARE + 1 : SPARE + 2, :] = y_own
    for r, row in ((2, x_own), (3, y_own)):
        hi, lo = split2(row)
        rest = (row - hi.astype(f32)) - lo.astype(f32)
        cur[0, SPARE + r : SPARE + r + 1, :] = rest

    def copy_of(stage, off, src_rank, dst_rank, target):
        return pltpu.make_async_remote_copy(
            src_ref=pay.at[stage, pl.ds(pl.multiple_of(src_rank * cap, cap), cap), :],
            dst_ref=recv.at[stage, pl.ds(pl.multiple_of(dst_rank * cap, cap), cap), :],
            send_sem=send_sem.at[stage, off],
            recv_sem=recv_sem.at[stage, off],
            device_id={"mesh": target},
            device_id_type=MESH,
        )

    def pack(stage, c):
        both = jnp.dot(lhs[c], hot_send[...], preferred_element_type=f32)
        pay[stage] = jnp.transpose(both[:ROWS] + both[ROWS:])

    def send(stage):
        for off in range(1, n_mesh):
            to = lax.rem(me + off, n_mesh)
            copy_of(stage, off, to, me, to).start()

    def own(stage):
        at = pl.ds(pl.multiple_of(me * cap, cap), cap)
        recv[stage, at, :] = pay[stage, at, :]

    def arrive(stage):
        for off in range(1, n_mesh):
            copy_of(stage, off, 0, me, lax.rem(me + off, n_mesh)).wait_recv()

    def ghosts_of(stage):
        hi, lo = split2(jnp.transpose(recv[stage]))
        return jnp.concatenate([hi, lo], axis=0)

    def split_chunk(c):
        hi, lo = split2(cur[c])
        lhs[c, 0:ROWS] = hi
        lhs[c, ROWS : 2 * ROWS] = lo

    for c in range(chunks):
        split_chunk(c)
        pack(c, c)

    expected = (n_mesh - 1) + (fi > 0).astype(jnp.int32) + (fi < n_freq - 1).astype(jnp.int32)
    pl.semaphore_wait(barrier, expected)
    for c in range(chunks):
        send(c)

    up_copy = pltpu.make_async_remote_copy(
        src_ref=spec_ref.at[pl.ds(band - REACH, REACH)], dst_ref=halo_lo,
        send_sem=halo_sem.at[0], recv_sem=halo_sem.at[1],
        device_id={"freq": lax.rem(fi + 1, n_freq)}, device_id_type=MESH,
    )
    down_copy = pltpu.make_async_remote_copy(
        src_ref=spec_ref.at[pl.ds(0, UP_REACH)], dst_ref=halo_hi,
        send_sem=halo_sem.at[2], recv_sem=halo_sem.at[3],
        device_id={"freq": lax.rem(fi + n_freq - 1, n_freq)}, device_id_type=MESH,
    )

    @pl.when(fi < n_freq - 1)
    def _():
        up_copy.start()

    @pl.when(fi > 0)
    def _():
        down_copy.start()

    @pl.when(fi == 0)
    def _():
        halo_lo[...] = jnp.zeros(halo_lo.shape, f32)

    @pl.when(fi == n_freq - 1)
    def _():
        halo_hi[...] = jnp.zeros(halo_hi.shape, f32)

    for c in range(chunks):
        own(c)

    def build(k, carry):
        entry = nb_ref[pl.ds(k, 1), :]
        rows = lax.broadcasted_iota(jnp.int32, (nodes + ghosts, nodes), 0)
        hot[k] = (rows == entry).astype(f32).astype(bf16)
        for c in range(chunks):
            both = jnp.dot(lhs[c], hot[k, 0:nodes], preferred_element_type=f32)
            picked[k, c] = both[:ROWS] + both[ROWS:]
        return carry

    lax.fori_loop(0, slots, build, 0)

    angle = (lax.broadcasted_iota(jnp.int32, (PITCH, 128), 0).astype(f32) + 0.5) * (
        2.0 * math.pi / dirs
    )
    real = lax.broadcasted_iota(jnp.int32, (PITCH, 128), 0) < dirs
    cosine = jnp.where(real, jnp.cos(angle), 0.0)[:, 0:1]
    sine = jnp.where(real, jnp.sin(angle), 0.0)[:, 0:1]
    ratios = []
    for j in range(band):
        value = jnp.float32(freq_ratio ** (j - NF // 2))
        for b in range(1, n_freq):
            value = jnp.where(fi == b, jnp.float32(freq_ratio ** (b * band + j - NF // 2)), value)
        ratios.append(value)

    @pl.when(fi > 0)
    def _():
        up_copy.wait_recv()

    @pl.when(fi < n_freq - 1)
    def _():
        down_copy.wait_recv()

    along = cosine[:dirs] * wind_ref[0:1, :] + sine[:dirs] * wind_ref[1:2, :]
    for j in range(band):
        own_bin = spec_ref[j]
        upper = spec_ref[j + UP_REACH] if j + UP_REACH < band else halo_hi[j + UP_REACH - band]
        lower = spec_ref[j - REACH] if j >= REACH else halo_lo[j]
        p1 = roll_rows(upper, -UP_SHIFT)
        m1 = roll_rows(lower, DOWN_SHIFT)
        p2 = roll_rows(upper, UP_SHIFT)
        m2 = roll_rows(lower, -DOWN_SHIFT)
        quad = quad_coupling * (
            own_bin * own_bin * (p1 + m1 + p2 + m2) - 2.0 * own_bin * (p1 * m1 + p2 * m2)
        )
        growth = wind_growth * jnp.maximum(along * ratios[j] - 1.0, 0.0)
        c, at = j // PER, (j % PER) * PITCH
        base[c, at : at + dirs, :] = own_bin + time_step * (quad + growth * own_bin)
        base[c, at + dirs : at + PITCH, :] = jnp.zeros((PITCH - dirs, nodes), f32)

    speeds = [group_scale / r for r in ratios]
    scale = time_step * inv_ref[...]

    def finish(c, j, store):
        at = j * PITCH
        speed = speeds[c * PER + j]
        store(
            (base[c, at : at + PITCH, :] + speed * acc[c, at : at + PITCH, :])
            / (1.0 + speed * wsum[...])
        )

    wsum[...] = jnp.zeros(wsum.shape, f32)

    for c in range(chunks):
        arrive(c)
        far = ghosts_of(c)
        acc[c] = jnp.zeros((SPARE, nodes), f32)

        def slot1(k, carry, c=c, far=far):
            both = jnp.dot(far, hot[k, nodes:], preferred_element_type=f32)
            value = picked[k, c] + (both[:ROWS] + both[ROWS:])
            if c == 0:
                dx = (value[SPARE : SPARE + 1] + value[SPARE + 2 : SPARE + 3]) - x_own
                dy = (value[SPARE + 1 : SPARE + 2] + value[SPARE + 3 : SPARE + 4]) - y_own
                w = scale * jnp.maximum(-(cosine * dx + sine * dy), 0.0)
                weights[k] = w
                wsum[...] += w
            else:
                w = weights[k]
            for j in range(PER):
                at = j * PITCH
                acc[c, at : at + PITCH, :] += w * value[at : at + PITCH]
            return carry

        lax.fori_loop(0, slots, slot1, 0)
        for j in range(PER):
            def store(v, c=c, at=j * PITCH):
                cur[c, at : at + PITCH, :] = v

            finish(c, j, store)
        split_chunk(c)
        pack(chunks + c, c)
        send(chunks + c)
        own(chunks + c)
        acc[c] = jnp.zeros((SPARE, nodes), f32)

        def local2(k, carry, c=c):
            both = jnp.dot(lhs[c], hot[k, 0:nodes], preferred_element_type=f32)
            w = weights[k]
            for j in range(PER):
                at = j * PITCH
                acc[c, at : at + PITCH, :] += w * (
                    both[at : at + PITCH] + both[ROWS + at : ROWS + at + PITCH]
                )
            return carry

        lax.fori_loop(0, slots, local2, 0)

    for c in range(chunks):
        arrive(chunks + c)
        far = ghosts_of(chunks + c)

        def slot2(k, carry, c=c, far=far):
            both = jnp.dot(far, hot[k, nodes:], preferred_element_type=f32)
            w = weights[k]
            for j in range(PER):
                at = j * PITCH
                acc[c, at : at + PITCH, :] += w * (
                    both[at : at + PITCH] + both[ROWS + at : ROWS + at + PITCH]
                )
            return carry

        lax.fori_loop(0, slots, slot2, 0)
        for j in range(PER):
            def store(v, f=c * PER + j):
                out_ref[f] = v[:dirs]

            finish(c, j, store)

    for stage in range(2 * chunks):
        for off in range(1, n_mesh):
            to = lax.rem(me + off, n_mesh)
            copy_of(stage, off, to, me, to).wait_send()

    @pl.when(fi < n_freq - 1)
    def _():
        up_copy.wait_send()

    @pl.when(fi > 0)
    def _():
        down_copy.wait_send()


def local(n_mesh, n_freq, spectra, coords, inv_area, wind_vector, neighbours, send_nodes, send_count):
    band, dirs, nodes = spectra.shape
    cap = send_nodes.shape[1]
    slots = neighbours.shape[0]
    ghosts = n_mesh * cap
    chunks = band // PER
    f32, bf16 = jnp.float32, jnp.bfloat16
    vmem = pl.BlockSpec(memory_space=pltpu.VMEM)
    return pl.pallas_call(
        functools.partial(kernel, n_mesh, n_freq, dirs, cap),
        out_shape=jax.ShapeDtypeStruct(spectra.shape, f32),
        in_specs=[vmem] * 6 + [pl.BlockSpec(memory_space=pltpu.SMEM)],
        out_specs=vmem,
        scratch_shapes=[
            pltpu.VMEM((chunks, ROWS, nodes), f32),
            pltpu.VMEM((chunks, 2 * ROWS, nodes), bf16),
            pltpu.VMEM((slots, chunks, ROWS, nodes), f32),
            pltpu.VMEM((chunks, SPARE, nodes), f32),
            pltpu.VMEM((chunks, SPARE, nodes), f32),
            pltpu.VMEM((slots, PITCH, nodes), f32),
            pltpu.VMEM((PITCH, nodes), f32),
            pltpu.VMEM((slots, nodes + ghosts, nodes), bf16),
            pltpu.VMEM((nodes, ghosts), bf16),
            pltpu.VMEM((2 * chunks, ghosts, ROWS), f32),
            pltpu.VMEM((2 * chunks, ghosts, ROWS), f32),
            pltpu.VMEM((REACH, dirs, nodes), f32),
            pltpu.VMEM((UP_REACH, dirs, nodes), f32),
            pltpu.SemaphoreType.DMA((2 * chunks, n_mesh)),
            pltpu.SemaphoreType.DMA((2 * chunks, n_mesh)),
            pltpu.SemaphoreType.DMA((4,)),
        ],
        compiler_params=pltpu.CompilerParams(
            collective_id=0, has_side_effects=True, vmem_limit_bytes=48 * 1024 * 1024
        ),
        cost_estimate=pl.CostEstimate(
            flops=4 * 2 * band * dirs * (nodes + ghosts) * nodes * slots,
            bytes_accessed=2 * 4 * band * dirs * nodes,
            transcendentals=0,
        ),
    )(spectra, coords, inv_area.reshape(1, nodes), wind_vector, neighbours, send_nodes, send_count)


def solution(mesh):
    in_specs = (
        P("freq", None, "mesh"),
        P(None, "mesh"),
        P("mesh"),
        P(None, "mesh"),
        P(None, "mesh"),
        P("mesh", None),
        P("mesh"),
    )
    return jax.shard_map(
        functools.partial(local, mesh.shape["mesh"], mesh.shape["freq"]),
        mesh=mesh, in_specs=in_specs, out_specs=P("freq", None, "mesh"), check_vma=False,
    )
```

```python
import functools
import math

import jax
import jax.numpy as jnp
from jax import lax
from jax.experimental import pallas as pl
from jax.experimental.pallas import tpu as pltpu
from jax.sharding import PartitionSpec as P

NF = 36
REACH = 3
UP_REACH = REACH - 1
UP_SHIFT = 1
DOWN_SHIFT = 3

time_step = 0.5
group_scale = 0.8
quad_coupling = 0.25
wind_growth = 0.1
freq_ratio = 1.1

MESH = pl.DeviceIdType.MESH
PER = 3
LANES = 128


def split2(x):
    hi = x.astype(jnp.bfloat16)
    lo = (x - hi.astype(jnp.float32)).astype(jnp.bfloat16)
    return hi, lo


def roll_rows(x, shift):
    count = x.shape[0]
    cut = (-shift) % count
    return jnp.concatenate([x[cut:], x[:cut]], axis=0)


def kernel(
    n_mesh, n_freq, dirs, cap,
    spec_hbm, coords_hbm, inv_hbm, wind_hbm, nb_hbm, send_hbm, count_hbm,
    out_ref,
    spec_ref, coords_ref, inv_ref, wind_ref, nb_ref, send_ref, count_ref,
    lhs, picked, base, acc, weights, hot, hot_send, pay, recv, halo_lo, halo_hi,
    in_sem, send_sem, recv_sem, halo_sem,
):
    band = spec_ref.shape[0]
    nodes = spec_ref.shape[2]
    slots = nb_ref.shape[0]
    ghosts = n_mesh * cap
    chunks = band // PER
    main = dirs // 8 * 8
    rest = dirs - main
    rows = lhs.shape[1] // 2
    tail = PER * main
    spare = tail + PER * rest
    tail_rows = rows - tail
    half = nodes // 2
    f32 = jnp.float32
    bf16 = jnp.bfloat16
    me = lax.axis_index("mesh")
    fi = lax.axis_index("freq")

    pairs = (
        (send_hbm, send_ref), (count_hbm, count_ref), (spec_hbm, spec_ref),
        (coords_hbm, coords_ref), (nb_hbm, nb_ref), (inv_hbm, inv_ref), (wind_hbm, wind_ref),
    )
    loads = [pltpu.make_async_copy(a, b, in_sem.at[i]) for i, (a, b) in enumerate(pairs)]
    for load in loads:
        load.start()

    barrier = pltpu.get_barrier_semaphore()
    for off in range(1, n_mesh):
        pl.semaphore_signal(
            barrier, inc=1, device_id={"mesh": lax.rem(me + off, n_mesh)}, device_id_type=MESH
        )

    @pl.when(fi > 0)
    def _():
        pl.semaphore_signal(barrier, inc=1, device_id={"freq": fi - 1}, device_id_type=MESH)

    @pl.when(fi < n_freq - 1)
    def _():
        pl.semaphore_signal(barrier, inc=1, device_id={"freq": fi + 1}, device_id_type=MESH)

    row_id = lax.broadcasted_iota(jnp.int32, (main + tail_rows, LANES), 0)
    direction = jnp.where(row_id < main, row_id, main + (row_id - main) % rest)
    angle = (direction.astype(f32) + 0.5) * (2.0 * math.pi / dirs)
    real = row_id < main + PER * rest
    cosine = jnp.where(real, jnp.cos(angle), 0.0)[:, 0:1]
    sine = jnp.where(real, jnp.sin(angle), 0.0)[:, 0:1]
    ratios = []
    for j in range(band):
        value = jnp.float32(freq_ratio ** (j - NF // 2))
        for b in range(1, n_freq):
            value = jnp.where(fi == b, jnp.float32(freq_ratio ** (b * band + j - NF // 2)), value)
        ratios.append(value)
    speeds = [group_scale / r for r in ratios]

    loads[0].wait()
    cells = send_ref[...].astype(f32)
    lane_c = lax.broadcasted_iota(jnp.int32, (cap, ghosts), 1) % cap
    spread = (lane_c == lax.broadcasted_iota(jnp.int32, (cap, ghosts), 0)).astype(f32)
    wide = jnp.dot(cells, spread, precision=lax.Precision.HIGHEST, preferred_element_type=f32)
    owner_lane = lax.broadcasted_iota(jnp.int32, (n_mesh, ghosts), 1) // cap
    mine = owner_lane == lax.broadcasted_iota(jnp.int32, (n_mesh, ghosts), 0)
    send_row = jnp.sum(jnp.where(mine, wide, 0.0), axis=0, keepdims=True)
    send_row = (send_row + 0.5).astype(jnp.int32)
    lane = lax.broadcasted_iota(jnp.int32, (1, ghosts), 1)
    limit = jnp.zeros((1, ghosts), jnp.int32)
    loads[1].wait()
    for d in range(n_mesh):
        limit = jnp.where(lane // cap == d, count_ref[d], limit)
    send_row = jnp.where(lane % cap < limit, send_row, -1)
    hot_send[...] = (
        (lax.broadcasted_iota(jnp.int32, (nodes, ghosts), 0) == send_row).astype(f32).astype(bf16)
    )

    def copy_of(stage, off, src_rank, dst_rank, target):
        return pltpu.make_async_remote_copy(
            src_ref=pay.at[stage, pl.ds(pl.multiple_of(src_rank * cap, cap), cap), :],
            dst_ref=recv.at[stage, pl.ds(pl.multiple_of(dst_rank * cap, cap), cap), :],
            send_sem=send_sem.at[stage, off],
            recv_sem=recv_sem.at[stage, off],
            device_id={"mesh": target},
            device_id_type=MESH,
        )

    def pack(stage, c):
        both = jnp.dot(lhs[c], hot_send[...], preferred_element_type=f32)
        value = both[:rows] + both[rows:]
        filler = jnp.zeros((LANES - rows, ghosts), f32)
        pay[stage] = jnp.transpose(jnp.concatenate([value, filler], axis=0))

    def send(stage):
        for off in range(1, n_mesh):
            to = lax.rem(me + off, n_mesh)
            copy_of(stage, off, to, me, to).start()

    def own(stage):
        at = pl.ds(pl.multiple_of(me * cap, cap), cap)
        recv[stage, at, :] = pay[stage, at, :]

    def arrive(stage):
        for off in range(1, n_mesh):
            copy_of(stage, off, 0, me, lax.rem(me + off, n_mesh)).wait_recv()

    def ghosts_of(stage):
        hi, lo = split2(jnp.transpose(recv[stage])[:rows])
        return jnp.concatenate([hi, lo], axis=0)

    def split_chunk(c, value):
        hi, lo = split2(value)
        lhs[c, 0:rows] = hi
        lhs[c, rows : 2 * rows] = lo

    loads[2].wait()
    loads[3].wait()
    x_own = coords_ref[0:1, :]
    y_own = coords_ref[1:2, :]
    remains = []
    for row in (x_own, y_own):
        hi, lo = split2(row)
        remains.append((row - hi.astype(f32)) - lo.astype(f32))
    for c in range(chunks):
        parts = [spec_ref[c * PER + j, 0:main, :] for j in range(PER)]
        parts += [spec_ref[c * PER + j, main:dirs, :] for j in range(PER)]
        if c == 0:
            parts += [x_own, y_own] + remains
        else:
            parts += [jnp.zeros((rows - spare, nodes), f32)]
        split_chunk(c, jnp.concatenate(parts, axis=0))
        pack(c, c)

    expected = (n_mesh - 1) + (fi > 0).astype(jnp.int32) + (fi < n_freq - 1).astype(jnp.int32)
    pl.semaphore_wait(barrier, expected)
    for c in range(chunks):
        send(c)

    up_copy = pltpu.make_async_remote_copy(
        src_ref=spec_ref.at[pl.ds(band - REACH, REACH)], dst_ref=halo_lo,
        send_sem=halo_sem.at[0], recv_sem=halo_sem.at[1],
        device_id={"freq": lax.rem(fi + 1, n_freq)}, device_id_type=MESH,
    )
    down_copy = pltpu.make_async_remote_copy(
        src_ref=spec_ref.at[pl.ds(0, UP_REACH)], dst_ref=halo_hi,
        send_sem=halo_sem.at[2], recv_sem=halo_sem.at[3],
        device_id={"freq": lax.rem(fi + n_freq - 1, n_freq)}, device_id_type=MESH,
    )

    @pl.when(fi < n_freq - 1)
    def _():
        up_copy.start()

    @pl.when(fi > 0)
    def _():
        down_copy.start()

    @pl.when(fi == 0)
    def _():
        halo_lo[...] = jnp.zeros(halo_lo.shape, f32)

    @pl.when(fi == n_freq - 1)
    def _():
        halo_hi[...] = jnp.zeros(halo_hi.shape, f32)

    for load in loads[4:]:
        load.wait()
    for c in range(chunks):
        own(c)

    def product(part, k, first, last, side):
        both = jnp.dot(
            part, hot[k, first:last, side * half : (side + 1) * half], preferred_element_type=f32
        )
        return both[:rows] + both[rows:]

    for k in range(slots):
        entry = nb_ref[k : k + 1, :]
        ids = lax.broadcasted_iota(jnp.int32, (nodes + ghosts, nodes), 0)
        hot[k] = (ids == entry).astype(f32).astype(bf16)
    for k in range(slots):
        for c in range(chunks):
            for side in range(2):
                lanes = slice(side * half, (side + 1) * half)
                picked[k, c, :, lanes] = product(lhs[c], k, 0, nodes, side)

    along = cosine[:main] * wind_ref[0:1, :] + sine[:main] * wind_ref[1:2, :]
    along_rest = (
        cosine[main : main + rest] * wind_ref[0:1, :] + sine[main : main + rest] * wind_ref[1:2, :]
    )
    along = jnp.concatenate([along, along_rest], axis=0)

    def sources(j):
        own_bin = spec_ref[j]
        upper = spec_ref[j + UP_REACH] if j + UP_REACH < band else halo_hi[j + UP_REACH - band]
        lower = spec_ref[j - REACH] if j >= REACH else halo_lo[j]
        p1 = roll_rows(upper, -UP_SHIFT)
        m1 = roll_rows(lower, DOWN_SHIFT)
        p2 = roll_rows(upper, UP_SHIFT)
        m2 = roll_rows(lower, -DOWN_SHIFT)
        quad = quad_coupling * (
            own_bin * own_bin * (p1 + m1 + p2 + m2) - 2.0 * own_bin * (p1 * m1 + p2 * m2)
        )
        growth = wind_growth * jnp.maximum(along * ratios[j] - 1.0, 0.0)
        value = own_bin + time_step * (quad + growth * own_bin)
        c, at = divmod(j, PER)
        base[c, at * main : (at + 1) * main, :] = value[:main]
        base[c, tail + at * rest : tail + (at + 1) * rest, :] = value[main:]

    for c in range(chunks):
        base[c, spare:rows, :] = jnp.zeros((rows - spare, nodes), f32)
    middle = range(REACH, band - UP_REACH)
    for j in middle:
        sources(j)

    @pl.when(fi > 0)
    def _():
        up_copy.wait_recv()

    @pl.when(fi < n_freq - 1)
    def _():
        down_copy.wait_recv()

    for j in range(band):
        if j not in middle:
            sources(j)

    scale = time_step * inv_ref[...]
    chunk_row = lax.broadcasted_iota(jnp.int32, (rows, LANES), 0)

    def speed_column(c):
        column = jnp.zeros((rows, LANES), f32)
        for j in range(PER):
            inside = (chunk_row >= j * main) & (chunk_row < (j + 1) * main)
            behind = (chunk_row >= tail + j * rest) & (chunk_row < tail + (j + 1) * rest)
            column = jnp.where(inside | behind, speeds[c * PER + j], column)
        return column[:, 0:1]

    def all_rows(w):
        return jnp.concatenate([w[:main]] * PER + [w[main:]], axis=0)

    def finish(c, lanes, total, column):
        wsum = weights[0, :, lanes]
        for k in range(1, slots):
            wsum = wsum + weights[k, :, lanes]
        return (base[c, :, lanes] + column * total) / (1.0 + column * all_rows(wsum))

    columns = [speed_column(c) for c in range(chunks)]
    for c in range(chunks):
        arrive(c)
        far = ghosts_of(c)
        for side in range(2):
            lanes = slice(side * half, (side + 1) * half)
            total = None
            for k in range(slots):
                value = picked[k, c, :, lanes] + product(far, k, nodes, nodes + ghosts, side)
                if c == 0:
                    dx = value[spare : spare + 1] + value[spare + 2 : spare + 3] - x_own[:, lanes]
                    dy = value[spare + 1 : spare + 2] + value[spare + 3 : spare + 4] - y_own[:, lanes]
                    w = scale[:, lanes] * jnp.maximum(-(cosine * dx + sine * dy), 0.0)
                    weights[k, :, lanes] = w
                else:
                    w = weights[k, :, lanes]
                term = all_rows(w) * value
                total = term if total is None else total + term
            value = finish(c, lanes, total, columns[c])
            hi, lo = split2(value)
            lhs[c, 0:rows, lanes] = hi
            lhs[c, rows : 2 * rows, lanes] = lo
        pack(chunks + c, c)
        send(chunks + c)
        own(chunks + c)
        for side in range(2):
            lanes = slice(side * half, (side + 1) * half)
            total = None
            for k in range(slots):
                term = all_rows(weights[k, :, lanes]) * product(lhs[c], k, 0, nodes, side)
                total = term if total is None else total + term
            acc[c, :, lanes] = total

    for c in range(chunks):
        arrive(chunks + c)
        far = ghosts_of(chunks + c)
        for side in range(2):
            lanes = slice(side * half, (side + 1) * half)
            total = acc[c, :, lanes]
            for k in range(slots):
                total = total + all_rows(weights[k, :, lanes]) * product(
                    far, k, nodes, nodes + ghosts, side
                )
            value = finish(c, lanes, total, columns[c])
            for j in range(PER):
                out_ref[c * PER + j, 0:main, lanes] = value[j * main : (j + 1) * main]
                at = tail + j * rest
                out_ref[c * PER + j, main:dirs, lanes] = value[at : at + rest]

    for stage in range(2 * chunks):
        for off in range(1, n_mesh):
            to = lax.rem(me + off, n_mesh)
            copy_of(stage, off, to, me, to).wait_send()

    @pl.when(fi < n_freq - 1)
    def _():
        up_copy.wait_send()

    @pl.when(fi > 0)
    def _():
        down_copy.wait_send()


def local(n_mesh, n_freq, spectra, coords, inv_area, wind_vector, neighbours, send_nodes, send_count):
    band, dirs, nodes = spectra.shape
    cap = send_nodes.shape[1]
    slots = neighbours.shape[0]
    ghosts = n_mesh * cap
    chunks = band // PER
    main = dirs // 8 * 8
    rows = PER * main + -(-(PER * (dirs - main) + 4) // 8) * 8
    f32, bf16, i32 = jnp.float32, jnp.bfloat16, jnp.int32
    hbm = pl.BlockSpec(memory_space=pltpu.HBM)
    return pl.pallas_call(
        functools.partial(kernel, n_mesh, n_freq, dirs, cap),
        out_shape=jax.ShapeDtypeStruct(spectra.shape, f32),
        in_specs=[hbm] * 7,
        out_specs=pl.BlockSpec(memory_space=pltpu.VMEM),
        scratch_shapes=[
            pltpu.VMEM(spectra.shape, f32),
            pltpu.VMEM(coords.shape, f32),
            pltpu.VMEM((1, nodes), f32),
            pltpu.VMEM(wind_vector.shape, f32),
            pltpu.VMEM(neighbours.shape, i32),
            pltpu.VMEM(send_nodes.shape, i32),
            pltpu.SMEM(send_count.shape, i32),
            pltpu.VMEM((chunks, 2 * rows, nodes), bf16),
            pltpu.VMEM((slots, chunks, rows, nodes), f32),
            pltpu.VMEM((chunks, rows, nodes), f32),
            pltpu.VMEM((chunks, rows, nodes), f32),
            pltpu.VMEM((slots, main + rows - PER * main, nodes), f32),
            pltpu.VMEM((slots, nodes + ghosts, nodes), bf16),
            pltpu.VMEM((nodes, ghosts), bf16),
            pltpu.VMEM((2 * chunks, ghosts, LANES), f32),
            pltpu.VMEM((2 * chunks, ghosts, LANES), f32),
            pltpu.VMEM((REACH, dirs, nodes), f32),
            pltpu.VMEM((UP_REACH, dirs, nodes), f32),
            pltpu.SemaphoreType.DMA((7,)),
            pltpu.SemaphoreType.DMA((2 * chunks, n_mesh)),
            pltpu.SemaphoreType.DMA((2 * chunks, n_mesh)),
            pltpu.SemaphoreType.DMA((4,)),
        ],
        compiler_params=pltpu.CompilerParams(
            collective_id=0, has_side_effects=True, vmem_limit_bytes=64 * 1024 * 1024
        ),
        cost_estimate=pl.CostEstimate(
            flops=4 * 2 * band * dirs * (nodes + ghosts) * nodes * slots,
            bytes_accessed=2 * 4 * band * dirs * nodes,
            transcendentals=0,
        ),
    )(spectra, coords, inv_area.reshape(1, nodes), wind_vector, neighbours, send_nodes, send_count)


def solution(mesh):
    in_specs = (
        P("freq", None, "mesh"),
        P(None, "mesh"),
        P("mesh"),
        P(None, "mesh"),
        P(None, "mesh"),
        P("mesh", None),
        P("mesh"),
    )
    return jax.shard_map(
        functools.partial(local, mesh.shape["mesh"], mesh.shape["freq"]),
        mesh=mesh, in_specs=in_specs, out_specs=P("freq", None, "mesh"), check_vma=False,
    )
```

```python
import functools
import math

import jax
import jax.numpy as jnp
from jax import lax
from jax.experimental import pallas as pl
from jax.experimental.pallas import tpu as pltpu
from jax.sharding import PartitionSpec as P

NF = 36
REACH = 3
UP_REACH = REACH - 1
UP_SHIFT = 1
DOWN_SHIFT = 3

time_step = 0.5
group_scale = 0.8
quad_coupling = 0.25
wind_growth = 0.1
freq_ratio = 1.1

MESH = pl.DeviceIdType.MESH
PER = 3
LANES = 128


def split2(x):
    hi = x.astype(jnp.bfloat16)
    lo = (x - hi.astype(jnp.float32)).astype(jnp.bfloat16)
    return hi, lo


def roll_rows(x, shift):
    count = x.shape[0]
    cut = (-shift) % count
    return jnp.concatenate([x[cut:], x[:cut]], axis=0)


def kernel(
    n_mesh, n_freq, dirs, cap,
    spec_hbm, coords_hbm, inv_hbm, wind_hbm, nb_hbm, send_hbm, count_hbm,
    out_hbm,
    out_ref, spec_ref, coords_ref, inv_ref, wind_ref, nb_ref, send_ref, count_ref,
    lhs, picked, base, acc, weights, hot, hot_send, pay, recv, halo_lo, halo_hi,
    in_sem, send_sem, recv_sem, halo_sem, out_sem,
):
    band = spec_ref.shape[0]
    nodes = spec_ref.shape[2]
    slots = nb_ref.shape[0]
    ghosts = n_mesh * cap
    chunks = band // PER
    main = dirs // 8 * 8
    rest = dirs - main
    rows = lhs.shape[1] // 2
    tail = PER * main
    spare = tail + PER * rest
    tail_rows = rows - tail
    half = nodes // 2
    groups = LANES // cap
    depth = rows // groups
    f32 = jnp.float32
    bf16 = jnp.bfloat16
    me = lax.axis_index("mesh")
    fi = lax.axis_index("freq")

    pairs = (
        (send_hbm, send_ref), (count_hbm, count_ref), (spec_hbm, spec_ref),
        (coords_hbm, coords_ref), (nb_hbm, nb_ref), (inv_hbm, inv_ref), (wind_hbm, wind_ref),
    )
    loads = [pltpu.make_async_copy(a, b, in_sem.at[i]) for i, (a, b) in enumerate(pairs)]
    for load in loads:
        load.start()

    barrier = pltpu.get_barrier_semaphore()
    for off in range(1, n_mesh):
        pl.semaphore_signal(
            barrier, inc=1, device_id={"mesh": lax.rem(me + off, n_mesh)}, device_id_type=MESH
        )

    @pl.when(fi > 0)
    def _():
        pl.semaphore_signal(barrier, inc=1, device_id={"freq": fi - 1}, device_id_type=MESH)

    @pl.when(fi < n_freq - 1)
    def _():
        pl.semaphore_signal(barrier, inc=1, device_id={"freq": fi + 1}, device_id_type=MESH)

    row_id = lax.broadcasted_iota(jnp.int32, (main + tail_rows, LANES), 0)
    direction = jnp.where(row_id < main, row_id, main + (row_id - main) % rest)
    angle = (direction.astype(f32) + 0.5) * (2.0 * math.pi / dirs)
    real = row_id < main + PER * rest
    cosine = jnp.where(real, jnp.cos(angle), 0.0)[:, 0:1]
    sine = jnp.where(real, jnp.sin(angle), 0.0)[:, 0:1]
    ratios = []
    for j in range(band):
        value = jnp.float32(freq_ratio ** (j - NF // 2))
        for b in range(1, n_freq):
            value = jnp.where(fi == b, jnp.float32(freq_ratio ** (b * band + j - NF // 2)), value)
        ratios.append(value)
    speeds = [group_scale / r for r in ratios]

    loads[0].wait()
    cells = send_ref[...].astype(f32)
    lane_c = lax.broadcasted_iota(jnp.int32, (cap, ghosts), 1) % cap
    spread = (lane_c == lax.broadcasted_iota(jnp.int32, (cap, ghosts), 0)).astype(f32)
    wide = jnp.dot(cells, spread, precision=lax.Precision.HIGHEST, preferred_element_type=f32)
    owner_lane = lax.broadcasted_iota(jnp.int32, (n_mesh, ghosts), 1) // cap
    mine = owner_lane == lax.broadcasted_iota(jnp.int32, (n_mesh, ghosts), 0)
    send_row = jnp.sum(jnp.where(mine, wide, 0.0), axis=0, keepdims=True)
    send_row = (send_row + 0.5).astype(jnp.int32)
    lane = lax.broadcasted_iota(jnp.int32, (1, ghosts), 1)
    limit = jnp.zeros((1, ghosts), jnp.int32)
    loads[1].wait()
    for d in range(n_mesh):
        limit = jnp.where(lane // cap == d, count_ref[d], limit)
    send_row = jnp.where(lane % cap < limit, send_row, -1)
    hot_send[...] = (
        (lax.broadcasted_iota(jnp.int32, (nodes, ghosts), 0) == send_row).astype(f32).astype(bf16)
    )

    def copy_of(stage, off, src_rank, dst_rank, target):
        return pltpu.make_async_remote_copy(
            src_ref=pay.at[stage, src_rank],
            dst_ref=recv.at[stage, dst_rank],
            send_sem=send_sem.at[stage, off],
            recv_sem=recv_sem.at[stage, off],
            device_id={"mesh": target},
            device_id_type=MESH,
        )

    def pack(stage, c):
        both = jnp.dot(lhs[c], hot_send[...], preferred_element_type=f32)
        value = both[:rows] + both[rows:]
        bands = [value[g * depth : (g + 1) * depth] for g in range(groups)]
        for d in range(n_mesh):
            pay[stage, d] = jnp.concatenate(
                [part[:, d * cap : (d + 1) * cap] for part in bands], axis=1
            )

    def send(stage):
        for off in range(1, n_mesh):
            to = lax.rem(me + off, n_mesh)
            copy_of(stage, off, to, me, to).start()

    def own(stage):
        recv[stage, me] = pay[stage, me]

    def arrive(stage):
        for off in range(1, n_mesh):
            copy_of(stage, off, 0, me, lax.rem(me + off, n_mesh)).wait_recv()

    def ghosts_of(stage):
        blocks = [recv[stage, d] for d in range(n_mesh)]
        bands = [
            jnp.concatenate([block[:, g * cap : (g + 1) * cap] for block in blocks], axis=1)
            for g in range(groups)
        ]
        hi, lo = split2(jnp.concatenate(bands, axis=0))
        return jnp.concatenate([hi, lo], axis=0)

    def split_chunk(c, value):
        hi, lo = split2(value)
        lhs[c, 0:rows] = hi
        lhs[c, rows : 2 * rows] = lo

    loads[2].wait()
    loads[3].wait()
    x_own = coords_ref[0:1, :]
    y_own = coords_ref[1:2, :]
    remains = []
    for row in (x_own, y_own):
        hi, lo = split2(row)
        remains.append((row - hi.astype(f32)) - lo.astype(f32))
    for c in range(chunks):
        parts = [spec_ref[c * PER + j, 0:main, :] for j in range(PER)]
        parts += [spec_ref[c * PER + j, main:dirs, :] for j in range(PER)]
        if c == 0:
            parts += [x_own, y_own] + remains
        else:
            parts += [jnp.zeros((rows - spare, nodes), f32)]
        split_chunk(c, jnp.concatenate(parts, axis=0))
        pack(c, c)
        if c == 0:
            expected = (n_mesh - 1) + (fi > 0).astype(jnp.int32)
            expected = expected + (fi < n_freq - 1).astype(jnp.int32)
            pl.semaphore_wait(barrier, expected)
        send(c)

    up_copy = pltpu.make_async_remote_copy(
        src_ref=spec_ref.at[pl.ds(band - REACH, REACH)], dst_ref=halo_lo,
        send_sem=halo_sem.at[0], recv_sem=halo_sem.at[1],
        device_id={"freq": lax.rem(fi + 1, n_freq)}, device_id_type=MESH,
    )
    down_copy = pltpu.make_async_remote_copy(
        src_ref=spec_ref.at[pl.ds(0, UP_REACH)], dst_ref=halo_hi,
        send_sem=halo_sem.at[2], recv_sem=halo_sem.at[3],
        device_id={"freq": lax.rem(fi + n_freq - 1, n_freq)}, device_id_type=MESH,
    )

    @pl.when(fi < n_freq - 1)
    def _():
        up_copy.start()

    @pl.when(fi > 0)
    def _():
        down_copy.start()

    @pl.when(fi == 0)
    def _():
        halo_lo[...] = jnp.zeros(halo_lo.shape, f32)

    @pl.when(fi == n_freq - 1)
    def _():
        halo_hi[...] = jnp.zeros(halo_hi.shape, f32)

    for load in loads[4:]:
        load.wait()
    for c in range(chunks):
        own(c)

    def product(part, k, first, last, side):
        both = jnp.dot(
            part, hot[k, first:last, side * half : (side + 1) * half], preferred_element_type=f32
        )
        return both[:rows] + both[rows:]

    for k in range(slots):
        entry = nb_ref[k : k + 1, :]
        ids = lax.broadcasted_iota(jnp.int32, (nodes + ghosts, nodes), 0)
        hot[k] = (ids == entry).astype(f32).astype(bf16)
    for k in range(slots):
        for c in range(chunks):
            for side in range(2):
                lanes = slice(side * half, (side + 1) * half)
                picked[k, c, :, lanes] = product(lhs[c], k, 0, nodes, side)

    along = cosine[:main] * wind_ref[0:1, :] + sine[:main] * wind_ref[1:2, :]
    along_rest = (
        cosine[main : main + rest] * wind_ref[0:1, :] + sine[main : main + rest] * wind_ref[1:2, :]
    )
    along = jnp.concatenate([along, along_rest], axis=0)

    def sources(j):
        own_bin = spec_ref[j]
        upper = spec_ref[j + UP_REACH] if j + UP_REACH < band else halo_hi[j + UP_REACH - band]
        lower = spec_ref[j - REACH] if j >= REACH else halo_lo[j]
        p1 = roll_rows(upper, -UP_SHIFT)
        m1 = roll_rows(lower, DOWN_SHIFT)
        p2 = roll_rows(upper, UP_SHIFT)
        m2 = roll_rows(lower, -DOWN_SHIFT)
        quad = quad_coupling * (
            own_bin * own_bin * (p1 + m1 + p2 + m2) - 2.0 * own_bin * (p1 * m1 + p2 * m2)
        )
        growth = wind_growth * jnp.maximum(along * ratios[j] - 1.0, 0.0)
        value = own_bin + time_step * (quad + growth * own_bin)
        c, at = divmod(j, PER)
        base[c, at * main : (at + 1) * main, :] = value[:main]
        base[c, tail + at * rest : tail + (at + 1) * rest, :] = value[main:]

    for c in range(chunks):
        base[c, spare:rows, :] = jnp.zeros((rows - spare, nodes), f32)
    middle = range(REACH, band - UP_REACH)
    for j in middle:
        sources(j)

    @pl.when(fi > 0)
    def _():
        up_copy.wait_recv()

    @pl.when(fi < n_freq - 1)
    def _():
        down_copy.wait_recv()

    for j in range(band):
        if j not in middle:
            sources(j)

    scale = time_step * inv_ref[...]
    chunk_row = lax.broadcasted_iota(jnp.int32, (rows, LANES), 0)

    def speed_column(c):
        column = jnp.zeros((rows, LANES), f32)
        for j in range(PER):
            inside = (chunk_row >= j * main) & (chunk_row < (j + 1) * main)
            behind = (chunk_row >= tail + j * rest) & (chunk_row < tail + (j + 1) * rest)
            column = jnp.where(inside | behind, speeds[c * PER + j], column)
        return column[:, 0:1]

    def all_rows(w):
        return jnp.concatenate([w[:main]] * PER + [w[main:]], axis=0)

    def finish(c, lanes, total, column):
        wsum = weights[0, :, lanes]
        for k in range(1, slots):
            wsum = wsum + weights[k, :, lanes]
        return (base[c, :, lanes] + column * total) / (1.0 + column * all_rows(wsum))

    columns = [speed_column(c) for c in range(chunks)]
    for c in range(chunks):
        arrive(c)
        far = ghosts_of(c)
        for side in range(2):
            lanes = slice(side * half, (side + 1) * half)
            total = None
            for k in range(slots):
                value = picked[k, c, :, lanes] + product(far, k, nodes, nodes + ghosts, side)
                if c == 0:
                    dx = value[spare : spare + 1] + value[spare + 2 : spare + 3] - x_own[:, lanes]
                    dy = value[spare + 1 : spare + 2] + value[spare + 3 : spare + 4] - y_own[:, lanes]
                    w = scale[:, lanes] * jnp.maximum(-(cosine * dx + sine * dy), 0.0)
                    weights[k, :, lanes] = w
                else:
                    w = weights[k, :, lanes]
                term = all_rows(w) * value
                total = term if total is None else total + term
            value = finish(c, lanes, total, columns[c])
            hi, lo = split2(value)
            lhs[c, 0:rows, lanes] = hi
            lhs[c, rows : 2 * rows, lanes] = lo
        pack(chunks + c, c)
        send(chunks + c)
        own(chunks + c)
        for side in range(2):
            lanes = slice(side * half, (side + 1) * half)
            total = None
            for k in range(slots):
                term = all_rows(weights[k, :, lanes]) * product(lhs[c], k, 0, nodes, side)
                total = term if total is None else total + term
            acc[c, :, lanes] = total

    def result_of(c):
        band_of = pl.ds(c * PER, PER)
        return pltpu.make_async_copy(out_ref.at[band_of], out_hbm.at[band_of], out_sem.at[c])

    for c in range(chunks):
        arrive(chunks + c)
        far = ghosts_of(chunks + c)
        for side in range(2):
            lanes = slice(side * half, (side + 1) * half)
            total = acc[c, :, lanes]
            for k in range(slots):
                total = total + all_rows(weights[k, :, lanes]) * product(
                    far, k, nodes, nodes + ghosts, side
                )
            value = finish(c, lanes, total, columns[c])
            for j in range(PER):
                out_ref[c * PER + j, 0:main, lanes] = value[j * main : (j + 1) * main]
                at = tail + j * rest
                out_ref[c * PER + j, main:dirs, lanes] = value[at : at + rest]
        result_of(c).start()

    for c in range(chunks):
        result_of(c).wait()
    for stage in range(2 * chunks):
        for off in range(1, n_mesh):
            to = lax.rem(me + off, n_mesh)
            copy_of(stage, off, to, me, to).wait_send()

    @pl.when(fi < n_freq - 1)
    def _():
        up_copy.wait_send()

    @pl.when(fi > 0)
    def _():
        down_copy.wait_send()


def local(n_mesh, n_freq, spectra, coords, inv_area, wind_vector, neighbours, send_nodes, send_count):
    band, dirs, nodes = spectra.shape
    cap = send_nodes.shape[1]
    slots = neighbours.shape[0]
    ghosts = n_mesh * cap
    chunks = band // PER
    main = dirs // 8 * 8
    rows = PER * main + -(-(PER * (dirs - main) + 4) // 8) * 8
    f32, bf16, i32 = jnp.float32, jnp.bfloat16, jnp.int32
    hbm = pl.BlockSpec(memory_space=pltpu.HBM)
    return pl.pallas_call(
        functools.partial(kernel, n_mesh, n_freq, dirs, cap),
        out_shape=jax.ShapeDtypeStruct(spectra.shape, f32),
        in_specs=[hbm] * 7,
        out_specs=hbm,
        scratch_shapes=[
            pltpu.VMEM(spectra.shape, f32),
            pltpu.VMEM(spectra.shape, f32),
            pltpu.VMEM(coords.shape, f32),
            pltpu.VMEM((1, nodes), f32),
            pltpu.VMEM(wind_vector.shape, f32),
            pltpu.VMEM(neighbours.shape, i32),
            pltpu.VMEM(send_nodes.shape, i32),
            pltpu.SMEM(send_count.shape, i32),
            pltpu.VMEM((chunks, 2 * rows, nodes), bf16),
            pltpu.VMEM((slots, chunks, rows, nodes), f32),
            pltpu.VMEM((chunks, rows, nodes), f32),
            pltpu.VMEM((chunks, rows, nodes), f32),
            pltpu.VMEM((slots, main + rows - PER * main, nodes), f32),
            pltpu.VMEM((slots, nodes + ghosts, nodes), bf16),
            pltpu.VMEM((nodes, ghosts), bf16),
            pltpu.VMEM((2 * chunks, n_mesh, rows * cap // LANES, LANES), f32),
            pltpu.VMEM((2 * chunks, n_mesh, rows * cap // LANES, LANES), f32),
            pltpu.VMEM((REACH, dirs, nodes), f32),
            pltpu.VMEM((UP_REACH, dirs, nodes), f32),
            pltpu.SemaphoreType.DMA((7,)),
            pltpu.SemaphoreType.DMA((2 * chunks, n_mesh)),
            pltpu.SemaphoreType.DMA((2 * chunks, n_mesh)),
            pltpu.SemaphoreType.DMA((4,)),
            pltpu.SemaphoreType.DMA((chunks,)),
        ],
        compiler_params=pltpu.CompilerParams(
            collective_id=0, has_side_effects=True, vmem_limit_bytes=64 * 1024 * 1024
        ),
        cost_estimate=pl.CostEstimate(
            flops=4 * 2 * band * dirs * (nodes + ghosts) * nodes * slots,
            bytes_accessed=2 * 4 * band * dirs * nodes,
            transcendentals=0,
        ),
    )(spectra, coords, inv_area.reshape(1, nodes), wind_vector, neighbours, send_nodes, send_count)


def solution(mesh):
    in_specs = (
        P("freq", None, "mesh"),
        P(None, "mesh"),
        P("mesh"),
        P(None, "mesh"),
        P(None, "mesh"),
        P("mesh", None),
        P("mesh"),
    )
    return jax.shard_map(
        functools.partial(local, mesh.shape["mesh"], mesh.shape["freq"]),
        mesh=mesh, in_specs=in_specs, out_specs=P("freq", None, "mesh"), check_vma=False,
    )
```

```python
import functools
import math

import jax
import jax.numpy as jnp
from jax import lax
from jax.experimental import pallas as pl
from jax.experimental.pallas import tpu as pltpu
from jax.sharding import PartitionSpec as P

NF = 36
REACH = 3
UP_REACH = REACH - 1
UP_SHIFT = 1
DOWN_SHIFT = 3

time_step = 0.5
group_scale = 0.8
quad_coupling = 0.25
wind_growth = 0.1
freq_ratio = 1.1

MESH = pl.DeviceIdType.MESH
PER = 3
LANES = 128


def split2(x):
    hi = x.astype(jnp.bfloat16)
    lo = (x - hi.astype(jnp.float32)).astype(jnp.bfloat16)
    return hi, lo


def roll_rows(x, shift):
    count = x.shape[0]
    cut = (-shift) % count
    return jnp.concatenate([x[cut:], x[:cut]], axis=0)


def kernel(
    n_mesh, n_freq, dirs, cap,
    spec_hbm, coords_hbm, inv_hbm, wind_hbm, nb_hbm, send_hbm, count_hbm,
    out_hbm,
    out_ref, spec_ref, coords_ref, inv_ref, wind_ref, nb_ref, send_ref, count_ref,
    lhs, picked, base, acc, weights, hot, hot_send, pay, recv, halo_lo, halo_hi,
    in_sem, send_sem, recv_sem, halo_sem, out_sem,
):
    band = spec_ref.shape[0]
    nodes = spec_ref.shape[2]
    slots = nb_ref.shape[0]
    ghosts = n_mesh * cap
    chunks = band // PER
    main = dirs // 8 * 8
    rest = dirs - main
    rows = lhs.shape[1] // 2
    tail = PER * main
    spare = tail + PER * rest
    tail_rows = rows - tail
    half = nodes // 2
    groups = LANES // cap
    depth = rows // groups
    f32 = jnp.float32
    bf16 = jnp.bfloat16
    me = lax.axis_index("mesh")
    fi = lax.axis_index("freq")

    pairs = (
        (send_hbm, send_ref), (count_hbm, count_ref), (spec_hbm, spec_ref),
        (coords_hbm, coords_ref), (nb_hbm, nb_ref), (inv_hbm, inv_ref), (wind_hbm, wind_ref),
    )
    loads = [pltpu.make_async_copy(a, b, in_sem.at[i]) for i, (a, b) in enumerate(pairs)]
    for load in loads:
        load.start()

    barrier = pltpu.get_barrier_semaphore()
    for off in range(1, n_mesh):
        pl.semaphore_signal(
            barrier, inc=1, device_id={"mesh": lax.rem(me + off, n_mesh)}, device_id_type=MESH
        )

    @pl.when(fi > 0)
    def _():
        pl.semaphore_signal(barrier, inc=1, device_id={"freq": fi - 1}, device_id_type=MESH)

    @pl.when(fi < n_freq - 1)
    def _():
        pl.semaphore_signal(barrier, inc=1, device_id={"freq": fi + 1}, device_id_type=MESH)

    row_id = lax.broadcasted_iota(jnp.int32, (main + tail_rows, LANES), 0)
    direction = jnp.where(row_id < main, row_id, main + (row_id - main) % rest)
    angle = (direction.astype(f32) + 0.5) * (2.0 * math.pi / dirs)
    real = row_id < main + PER * rest
    cosine = jnp.where(real, jnp.cos(angle), 0.0)[:, 0:1]
    sine = jnp.where(real, jnp.sin(angle), 0.0)[:, 0:1]
    ratios = []
    for j in range(band):
        value = jnp.float32(freq_ratio ** (j - NF // 2))
        for b in range(1, n_freq):
            value = jnp.where(fi == b, jnp.float32(freq_ratio ** (b * band + j - NF // 2)), value)
        ratios.append(value)
    speeds = [group_scale / r for r in ratios]

    loads[0].wait()
    send_row = jnp.concatenate([send_ref[d : d + 1, :] for d in range(n_mesh)], axis=1)
    lane = lax.broadcasted_iota(jnp.int32, (1, ghosts), 1)
    limit = jnp.zeros((1, ghosts), jnp.int32)
    loads[1].wait()
    for d in range(n_mesh):
        limit = jnp.where(lane // cap == d, count_ref[d], limit)
    send_row = jnp.where(lane % cap < limit, send_row, -1)
    hot_send[...] = (
        (lax.broadcasted_iota(jnp.int32, (nodes, ghosts), 0) == send_row).astype(f32).astype(bf16)
    )

    def copy_of(stage, off, src_rank, dst_rank, target):
        return pltpu.make_async_remote_copy(
            src_ref=pay.at[stage, src_rank],
            dst_ref=recv.at[stage, dst_rank],
            send_sem=send_sem.at[stage, off],
            recv_sem=recv_sem.at[stage, off],
            device_id={"mesh": target},
            device_id_type=MESH,
        )

    def pack(stage, c):
        both = jnp.dot(lhs[c], hot_send[...], preferred_element_type=f32)
        value = both[:rows] + both[rows:]
        bands = [value[g * depth : (g + 1) * depth] for g in range(groups)]
        for d in range(n_mesh):
            pay[stage, d] = jnp.concatenate(
                [part[:, d * cap : (d + 1) * cap] for part in bands], axis=1
            )

    def send(stage):
        for off in range(1, n_mesh):
            to = lax.rem(me + off, n_mesh)
            copy_of(stage, off, to, me, to).start()

    def own(stage):
        recv[stage, me] = pay[stage, me]

    def arrive(stage):
        for off in range(1, n_mesh):
            copy_of(stage, off, 0, me, lax.rem(me + off, n_mesh)).wait_recv()

    def ghosts_of(stage):
        blocks = [recv[stage, d] for d in range(n_mesh)]
        bands = [
            jnp.concatenate([block[:, g * cap : (g + 1) * cap] for block in blocks], axis=1)
            for g in range(groups)
        ]
        hi, lo = split2(jnp.concatenate(bands, axis=0))
        return jnp.concatenate([hi, lo], axis=0)

    def split_chunk(c, value):
        hi, lo = split2(value)
        lhs[c, 0:rows] = hi
        lhs[c, rows : 2 * rows] = lo

    loads[2].wait()
    loads[3].wait()
    x_own = coords_ref[0:1, :]
    y_own = coords_ref[1:2, :]
    remains = []
    for row in (x_own, y_own):
        hi, lo = split2(row)
        remains.append((row - hi.astype(f32)) - lo.astype(f32))
    for c in range(chunks):
        parts = [spec_ref[c * PER + j, 0:main, :] for j in range(PER)]
        parts += [spec_ref[c * PER + j, main:dirs, :] for j in range(PER)]
        if c == 0:
            parts += [x_own, y_own] + remains
        else:
            parts += [jnp.zeros((rows - spare, nodes), f32)]
        split_chunk(c, jnp.concatenate(parts, axis=0))
        pack(c, c)
        if c == 0:
            expected = (n_mesh - 1) + (fi > 0).astype(jnp.int32)
            expected = expected + (fi < n_freq - 1).astype(jnp.int32)
            pl.semaphore_wait(barrier, expected)
        send(c)

    up_copy = pltpu.make_async_remote_copy(
        src_ref=spec_ref.at[pl.ds(band - REACH, REACH)], dst_ref=halo_lo,
        send_sem=halo_sem.at[0], recv_sem=halo_sem.at[1],
        device_id={"freq": lax.rem(fi + 1, n_freq)}, device_id_type=MESH,
    )
    down_copy = pltpu.make_async_remote_copy(
        src_ref=spec_ref.at[pl.ds(0, UP_REACH)], dst_ref=halo_hi,
        send_sem=halo_sem.at[2], recv_sem=halo_sem.at[3],
        device_id={"freq": lax.rem(fi + n_freq - 1, n_freq)}, device_id_type=MESH,
    )

    @pl.when(fi < n_freq - 1)
    def _():
        up_copy.start()

    @pl.when(fi > 0)
    def _():
        down_copy.start()

    @pl.when(fi == 0)
    def _():
        halo_lo[...] = jnp.zeros(halo_lo.shape, f32)

    @pl.when(fi == n_freq - 1)
    def _():
        halo_hi[...] = jnp.zeros(halo_hi.shape, f32)

    for load in loads[4:]:
        load.wait()
    for c in range(chunks):
        own(c)

    def product(part, k, first, last, side):
        both = jnp.dot(
            part, hot[k, first:last, side * half : (side + 1) * half], preferred_element_type=f32
        )
        return both[:rows] + both[rows:]

    along = cosine[:main] * wind_ref[0:1, :] + sine[:main] * wind_ref[1:2, :]
    along_rest = (
        cosine[main : main + rest] * wind_ref[0:1, :] + sine[main : main + rest] * wind_ref[1:2, :]
    )
    along = jnp.concatenate([along, along_rest], axis=0)

    def sources(j):
        own_bin = spec_ref[j]
        upper = spec_ref[j + UP_REACH] if j + UP_REACH < band else halo_hi[j + UP_REACH - band]
        lower = spec_ref[j - REACH] if j >= REACH else halo_lo[j]
        p1 = roll_rows(upper, -UP_SHIFT)
        m1 = roll_rows(lower, DOWN_SHIFT)
        p2 = roll_rows(upper, UP_SHIFT)
        m2 = roll_rows(lower, -DOWN_SHIFT)
        quad = quad_coupling * (
            own_bin * own_bin * (p1 + m1 + p2 + m2) - 2.0 * own_bin * (p1 * m1 + p2 * m2)
        )
        growth = wind_growth * jnp.maximum(along * ratios[j] - 1.0, 0.0)
        value = own_bin + time_step * (quad + growth * own_bin)
        c, at = divmod(j, PER)
        base[c, at * main : (at + 1) * main, :] = value[:main]
        base[c, tail + at * rest : tail + (at + 1) * rest, :] = value[main:]

    for c in range(chunks):
        base[c, spare:rows, :] = jnp.zeros((rows - spare, nodes), f32)

    def hot_columns(k):
        entry = nb_ref[k : k + 1, :]
        ids = lax.broadcasted_iota(jnp.int32, (nodes + ghosts, nodes), 0)
        hot[k] = (ids == entry).astype(f32).astype(bf16)

    def pick_local(k):
        every = lhs[...].reshape(chunks * 2 * rows, nodes)
        for side in range(2):
            lanes = slice(side * half, (side + 1) * half)
            both = jnp.dot(every, hot[k, 0:nodes, lanes], preferred_element_type=f32)
            for c in range(chunks):
                at = c * 2 * rows
                picked[k, c, :, lanes] = both[at : at + rows] + both[at + rows : at + 2 * rows]

    middle = list(range(REACH, band - UP_REACH))
    outer = [j for j in range(band) if j not in middle]
    first = slots // 2
    hot_columns(0)
    for k in range(slots):
        if k == first:
            @pl.when(fi > 0)
            def _():
                up_copy.wait_recv()

            @pl.when(fi < n_freq - 1)
            def _():
                down_copy.wait_recv()

        if k + 1 < slots:
            hot_columns(k + 1)
        pick_local(k)
        if k < first:
            for j in middle[k::first]:
                sources(j)
        else:
            for j in outer[k - first :: slots - first]:
                sources(j)

    scale = time_step * inv_ref[...]
    chunk_row = lax.broadcasted_iota(jnp.int32, (rows, LANES), 0)

    def speed_column(c):
        column = jnp.zeros((rows, LANES), f32)
        for j in range(PER):
            inside = (chunk_row >= j * main) & (chunk_row < (j + 1) * main)
            behind = (chunk_row >= tail + j * rest) & (chunk_row < tail + (j + 1) * rest)
            column = jnp.where(inside | behind, speeds[c * PER + j], column)
        return column[:, 0:1]

    def all_rows(w):
        return jnp.concatenate([w[:main]] * PER + [w[main:]], axis=0)

    def finish(c, lanes, total, column):
        wsum = weights[0, :, lanes]
        for k in range(1, slots):
            wsum = wsum + weights[k, :, lanes]
        return (base[c, :, lanes] + column * total) / (1.0 + column * all_rows(wsum))

    columns = [speed_column(c) for c in range(chunks)]
    for c in range(chunks):
        arrive(c)
        far = ghosts_of(c)
        for side in range(2):
            lanes = slice(side * half, (side + 1) * half)
            total = None
            for k in range(slots):
                value = picked[k, c, :, lanes] + product(far, k, nodes, nodes + ghosts, side)
                if c == 0:
                    dx = value[spare : spare + 1] + value[spare + 2 : spare + 3] - x_own[:, lanes]
                    dy = value[spare + 1 : spare + 2] + value[spare + 3 : spare + 4] - y_own[:, lanes]
                    w = scale[:, lanes] * jnp.maximum(-(cosine * dx + sine * dy), 0.0)
                    weights[k, :, lanes] = w
                else:
                    w = weights[k, :, lanes]
                term = all_rows(w) * value
                total = term if total is None else total + term
            value = finish(c, lanes, total, columns[c])
            hi, lo = split2(value)
            lhs[c, 0:rows, lanes] = hi
            lhs[c, rows : 2 * rows, lanes] = lo
        pack(chunks + c, c)
        send(chunks + c)
        own(chunks + c)
        for side in range(2):
            lanes = slice(side * half, (side + 1) * half)
            total = None
            for k in range(slots):
                term = all_rows(weights[k, :, lanes]) * product(lhs[c], k, 0, nodes, side)
                total = term if total is None else total + term
            acc[c, :, lanes] = total

    def result_of(c):
        band_of = pl.ds(c * PER, PER)
        return pltpu.make_async_copy(out_ref.at[band_of], out_hbm.at[band_of], out_sem.at[c])

    for c in range(chunks):
        arrive(chunks + c)
        far = ghosts_of(chunks + c)
        for side in range(2):
            lanes = slice(side * half, (side + 1) * half)
            total = acc[c, :, lanes]
            for k in range(slots):
                total = total + all_rows(weights[k, :, lanes]) * product(
                    far, k, nodes, nodes + ghosts, side
                )
            value = finish(c, lanes, total, columns[c])
            for j in range(PER):
                out_ref[c * PER + j, 0:main, lanes] = value[j * main : (j + 1) * main]
                at = tail + j * rest
                out_ref[c * PER + j, main:dirs, lanes] = value[at : at + rest]
        result_of(c).start()

    for c in range(chunks):
        result_of(c).wait()
    for stage in range(2 * chunks):
        for off in range(1, n_mesh):
            to = lax.rem(me + off, n_mesh)
            copy_of(stage, off, to, me, to).wait_send()

    @pl.when(fi < n_freq - 1)
    def _():
        up_copy.wait_send()

    @pl.when(fi > 0)
    def _():
        down_copy.wait_send()


def local(n_mesh, n_freq, spectra, coords, inv_area, wind_vector, neighbours, send_nodes, send_count):
    band, dirs, nodes = spectra.shape
    cap = send_nodes.shape[1]
    slots = neighbours.shape[0]
    ghosts = n_mesh * cap
    chunks = band // PER
    main = dirs // 8 * 8
    rows = PER * main + -(-(PER * (dirs - main) + 4) // 8) * 8
    f32, bf16, i32 = jnp.float32, jnp.bfloat16, jnp.int32
    hbm = pl.BlockSpec(memory_space=pltpu.HBM)
    return pl.pallas_call(
        functools.partial(kernel, n_mesh, n_freq, dirs, cap),
        out_shape=jax.ShapeDtypeStruct(spectra.shape, f32),
        in_specs=[hbm] * 7,
        out_specs=hbm,
        scratch_shapes=[
            pltpu.VMEM(spectra.shape, f32),
            pltpu.VMEM(spectra.shape, f32),
            pltpu.VMEM(coords.shape, f32),
            pltpu.VMEM((1, nodes), f32),
            pltpu.VMEM(wind_vector.shape, f32),
            pltpu.VMEM(neighbours.shape, i32),
            pltpu.VMEM(send_nodes.shape, i32),
            pltpu.SMEM(send_count.shape, i32),
            pltpu.VMEM((chunks, 2 * rows, nodes), bf16),
            pltpu.VMEM((slots, chunks, rows, nodes), f32),
            pltpu.VMEM((chunks, rows, nodes), f32),
            pltpu.VMEM((chunks, rows, nodes), f32),
            pltpu.VMEM((slots, main + rows - PER * main, nodes), f32),
            pltpu.VMEM((slots, nodes + ghosts, nodes), bf16),
            pltpu.VMEM((nodes, ghosts), bf16),
            pltpu.VMEM((2 * chunks, n_mesh, rows * cap // LANES, LANES), f32),
            pltpu.VMEM((2 * chunks, n_mesh, rows * cap // LANES, LANES), f32),
            pltpu.VMEM((REACH, dirs, nodes), f32),
            pltpu.VMEM((UP_REACH, dirs, nodes), f32),
            pltpu.SemaphoreType.DMA((7,)),
            pltpu.SemaphoreType.DMA((2 * chunks, n_mesh)),
            pltpu.SemaphoreType.DMA((2 * chunks, n_mesh)),
            pltpu.SemaphoreType.DMA((4,)),
            pltpu.SemaphoreType.DMA((chunks,)),
        ],
        compiler_params=pltpu.CompilerParams(
            collective_id=0, has_side_effects=True, vmem_limit_bytes=64 * 1024 * 1024
        ),
        cost_estimate=pl.CostEstimate(
            flops=4 * 2 * band * dirs * (nodes + ghosts) * nodes * slots,
            bytes_accessed=2 * 4 * band * dirs * nodes,
            transcendentals=0,
        ),
    )(spectra, coords, inv_area.reshape(1, nodes), wind_vector, neighbours, send_nodes, send_count)


def solution(mesh):
    in_specs = (
        P("freq", None, "mesh"),
        P(None, "mesh"),
        P("mesh"),
        P(None, "mesh"),
        P(None, "mesh"),
        P("mesh", None),
        P("mesh"),
    )
    return jax.shard_map(
        functools.partial(local, mesh.shape["mesh"], mesh.shape["freq"]),
        mesh=mesh, in_specs=in_specs, out_specs=P("freq", None, "mesh"), check_vma=False,
    )
```

```python
import functools
import math

import jax
import jax.numpy as jnp
from jax import lax
from jax.experimental import pallas as pl
from jax.experimental.pallas import tpu as pltpu
from jax.sharding import PartitionSpec as P

NF = 36
REACH = 3
UP_REACH = REACH - 1
UP_SHIFT = 1
DOWN_SHIFT = 3

time_step = 0.5
group_scale = 0.8
quad_coupling = 0.25
wind_growth = 0.1
freq_ratio = 1.1

MESH = pl.DeviceIdType.MESH
PER = 3
LANES = 128


def split2(x):
    hi = x.astype(jnp.bfloat16)
    lo = (x - hi.astype(jnp.float32)).astype(jnp.bfloat16)
    return hi, lo


def roll_rows(x, shift):
    count = x.shape[0]
    cut = (-shift) % count
    return jnp.concatenate([x[cut:], x[:cut]], axis=0)


def kernel(
    n_mesh, n_freq, dirs, cap,
    spec_hbm, coords_hbm, inv_hbm, wind_hbm, nb_hbm, send_hbm, count_hbm,
    out_hbm,
    out_ref, spec_ref, coords_ref, inv_ref, wind_ref, nb_ref, send_ref, count_ref,
    lhs, picked, base, acc, shares, weights, hot, hot_send, pay, recv, halo_lo, halo_hi,
    in_sem, send_sem, recv_sem, halo_sem, out_sem,
):
    band = spec_ref.shape[0]
    nodes = spec_ref.shape[2]
    slots = nb_ref.shape[0]
    ghosts = n_mesh * cap
    chunks = band // PER
    main = dirs // 8 * 8
    rest = dirs - main
    rows = lhs.shape[1] // 2
    tail = PER * main
    spare = tail + PER * rest
    tail_rows = rows - tail
    half = nodes // 2
    groups = LANES // cap
    depth = rows // groups
    f32 = jnp.float32
    bf16 = jnp.bfloat16
    me = lax.axis_index("mesh")
    fi = lax.axis_index("freq")

    pairs = (
        (send_hbm, send_ref), (count_hbm, count_ref), (spec_hbm, spec_ref),
        (coords_hbm, coords_ref), (nb_hbm, nb_ref), (inv_hbm, inv_ref), (wind_hbm, wind_ref),
    )
    loads = [pltpu.make_async_copy(a, b, in_sem.at[i]) for i, (a, b) in enumerate(pairs)]
    for load in loads:
        load.start()

    barrier = pltpu.get_barrier_semaphore()
    for off in range(1, n_mesh):
        pl.semaphore_signal(
            barrier, inc=1, device_id={"mesh": lax.rem(me + off, n_mesh)}, device_id_type=MESH
        )

    @pl.when(fi > 0)
    def _():
        pl.semaphore_signal(barrier, inc=1, device_id={"freq": fi - 1}, device_id_type=MESH)

    @pl.when(fi < n_freq - 1)
    def _():
        pl.semaphore_signal(barrier, inc=1, device_id={"freq": fi + 1}, device_id_type=MESH)

    row_id = lax.broadcasted_iota(jnp.int32, (main + tail_rows, LANES), 0)
    direction = jnp.where(row_id < main, row_id, main + (row_id - main) % rest)
    angle = (direction.astype(f32) + 0.5) * (2.0 * math.pi / dirs)
    real = row_id < main + PER * rest
    cosine = jnp.where(real, jnp.cos(angle), 0.0)[:, 0:1]
    sine = jnp.where(real, jnp.sin(angle), 0.0)[:, 0:1]
    ratios = []
    for j in range(band):
        value = jnp.float32(freq_ratio ** (j - NF // 2))
        for b in range(1, n_freq):
            value = jnp.where(fi == b, jnp.float32(freq_ratio ** (b * band + j - NF // 2)), value)
        ratios.append(value)
    speeds = [group_scale / r for r in ratios]

    loads[0].wait()
    send_row = jnp.concatenate([send_ref[d : d + 1, :] for d in range(n_mesh)], axis=1)
    lane = lax.broadcasted_iota(jnp.int32, (1, ghosts), 1)
    limit = jnp.zeros((1, ghosts), jnp.int32)
    loads[1].wait()
    for d in range(n_mesh):
        limit = jnp.where(lane // cap == d, count_ref[d], limit)
    send_row = jnp.where(lane % cap < limit, send_row, -1)
    hot_send[...] = (
        (lax.broadcasted_iota(jnp.int32, (nodes, ghosts), 0) == send_row).astype(f32).astype(bf16)
    )

    def copy_of(stage, off, src_rank, dst_rank, target):
        return pltpu.make_async_remote_copy(
            src_ref=pay.at[stage, src_rank],
            dst_ref=recv.at[stage, dst_rank],
            send_sem=send_sem.at[stage, off],
            recv_sem=recv_sem.at[stage, off],
            device_id={"mesh": target},
            device_id_type=MESH,
        )

    def pack(stage, c):
        both = jnp.dot(lhs[c], hot_send[...], preferred_element_type=f32)
        value = both[:rows] + both[rows:]
        bands = [value[g * depth : (g + 1) * depth] for g in range(groups)]
        for d in range(n_mesh):
            pay[stage, d] = jnp.concatenate(
                [part[:, d * cap : (d + 1) * cap] for part in bands], axis=1
            )

    def send(stage):
        for off in range(1, n_mesh):
            to = lax.rem(me + off, n_mesh)
            copy_of(stage, off, to, me, to).start()

    def own(stage):
        recv[stage, me] = pay[stage, me]

    def arrive(stage):
        for off in range(1, n_mesh):
            copy_of(stage, off, 0, me, lax.rem(me + off, n_mesh)).wait_recv()

    def ghosts_of(stage):
        blocks = [recv[stage, d] for d in range(n_mesh)]
        bands = [
            jnp.concatenate([block[:, g * cap : (g + 1) * cap] for block in blocks], axis=1)
            for g in range(groups)
        ]
        hi, lo = split2(jnp.concatenate(bands, axis=0))
        return jnp.concatenate([hi, lo], axis=0)

    def split_chunk(c, value):
        hi, lo = split2(value)
        lhs[c, 0:rows] = hi
        lhs[c, rows : 2 * rows] = lo

    loads[2].wait()
    loads[3].wait()
    x_own = coords_ref[0:1, :]
    y_own = coords_ref[1:2, :]
    remains = []
    for row in (x_own, y_own):
        hi, lo = split2(row)
        remains.append((row - hi.astype(f32)) - lo.astype(f32))
    for c in range(chunks):
        parts = [spec_ref[c * PER + j, 0:main, :] for j in range(PER)]
        parts += [spec_ref[c * PER + j, main:dirs, :] for j in range(PER)]
        if c == 0:
            parts += [x_own, y_own] + remains
        else:
            parts += [jnp.zeros((rows - spare, nodes), f32)]
        split_chunk(c, jnp.concatenate(parts, axis=0))
        pack(c, c)
        if c == 0:
            expected = (n_mesh - 1) + (fi > 0).astype(jnp.int32)
            expected = expected + (fi < n_freq - 1).astype(jnp.int32)
            pl.semaphore_wait(barrier, expected)
        send(c)

    up_copy = pltpu.make_async_remote_copy(
        src_ref=spec_ref.at[pl.ds(band - REACH, REACH)], dst_ref=halo_lo,
        send_sem=halo_sem.at[0], recv_sem=halo_sem.at[1],
        device_id={"freq": lax.rem(fi + 1, n_freq)}, device_id_type=MESH,
    )
    down_copy = pltpu.make_async_remote_copy(
        src_ref=spec_ref.at[pl.ds(0, UP_REACH)], dst_ref=halo_hi,
        send_sem=halo_sem.at[2], recv_sem=halo_sem.at[3],
        device_id={"freq": lax.rem(fi + n_freq - 1, n_freq)}, device_id_type=MESH,
    )

    @pl.when(fi < n_freq - 1)
    def _():
        up_copy.start()

    @pl.when(fi > 0)
    def _():
        down_copy.start()

    @pl.when(fi == 0)
    def _():
        halo_lo[...] = jnp.zeros(halo_lo.shape, f32)

    @pl.when(fi == n_freq - 1)
    def _():
        halo_hi[...] = jnp.zeros(halo_hi.shape, f32)

    for load in loads[4:]:
        load.wait()
    for c in range(chunks):
        own(c)

    def product(part, k, first, last, side):
        both = jnp.dot(
            part, hot[k, first:last, side * half : (side + 1) * half], preferred_element_type=f32
        )
        return both[:rows] + both[rows:]

    along = cosine[:main] * wind_ref[0:1, :] + sine[:main] * wind_ref[1:2, :]
    along_rest = (
        cosine[main : main + rest] * wind_ref[0:1, :] + sine[main : main + rest] * wind_ref[1:2, :]
    )
    along = jnp.concatenate([along, along_rest], axis=0)

    def sources(j):
        own_bin = spec_ref[j]
        upper = spec_ref[j + UP_REACH] if j + UP_REACH < band else halo_hi[j + UP_REACH - band]
        lower = spec_ref[j - REACH] if j >= REACH else halo_lo[j]
        p1 = roll_rows(upper, -UP_SHIFT)
        m1 = roll_rows(lower, DOWN_SHIFT)
        p2 = roll_rows(upper, UP_SHIFT)
        m2 = roll_rows(lower, -DOWN_SHIFT)
        quad = quad_coupling * (
            own_bin * own_bin * (p1 + m1 + p2 + m2) - 2.0 * own_bin * (p1 * m1 + p2 * m2)
        )
        growth = wind_growth * jnp.maximum(along * ratios[j] - 1.0, 0.0)
        value = own_bin + time_step * (quad + growth * own_bin)
        c, at = divmod(j, PER)
        base[c, at * main : (at + 1) * main, :] = value[:main]
        base[c, tail + at * rest : tail + (at + 1) * rest, :] = value[main:]

    for c in range(chunks):
        base[c, spare:rows, :] = jnp.zeros((rows - spare, nodes), f32)

    def hot_columns(k):
        entry = nb_ref[k : k + 1, :]
        ids = lax.broadcasted_iota(jnp.int32, (nodes + ghosts, nodes), 0)
        hot[k] = (ids == entry).astype(f32).astype(bf16)

    def pick_local(k):
        every = lhs[...].reshape(chunks * 2 * rows, nodes)
        for side in range(2):
            lanes = slice(side * half, (side + 1) * half)
            both = jnp.dot(every, hot[k, 0:nodes, lanes], preferred_element_type=f32)
            for c in range(chunks):
                at = c * 2 * rows
                picked[k, c, :, lanes] = both[at : at + rows] + both[at + rows : at + 2 * rows]

    middle = list(range(REACH, band - UP_REACH))
    outer = [j for j in range(band) if j not in middle]
    first = slots // 2
    hot_columns(0)
    for k in range(slots):
        if k == first:
            @pl.when(fi > 0)
            def _():
                up_copy.wait_recv()

            @pl.when(fi < n_freq - 1)
            def _():
                down_copy.wait_recv()

        if k + 1 < slots:
            hot_columns(k + 1)
        pick_local(k)
        if k < first:
            for j in middle[k::first]:
                sources(j)
        else:
            for j in outer[k - first :: slots - first]:
                sources(j)

    scale = time_step * inv_ref[...]
    chunk_row = lax.broadcasted_iota(jnp.int32, (rows, LANES), 0)

    def speed_column(c):
        column = jnp.zeros((rows, LANES), f32)
        for j in range(PER):
            inside = (chunk_row >= j * main) & (chunk_row < (j + 1) * main)
            behind = (chunk_row >= tail + j * rest) & (chunk_row < tail + (j + 1) * rest)
            column = jnp.where(inside | behind, speeds[c * PER + j], column)
        return column[:, 0:1]

    def all_rows(w):
        return jnp.concatenate([w[:main]] * PER + [w[main:]], axis=0)

    def divisor(lanes, column):
        wsum = weights[0, :, lanes]
        for k in range(1, slots):
            wsum = wsum + weights[k, :, lanes]
        return 1.0 / (1.0 + column * all_rows(wsum))

    columns = [speed_column(c) for c in range(chunks)]
    for c in range(chunks):
        arrive(c)
        far = ghosts_of(c)
        for side in range(2):
            lanes = slice(side * half, (side + 1) * half)
            total = None
            for k in range(slots):
                value = picked[k, c, :, lanes] + product(far, k, nodes, nodes + ghosts, side)
                if c == 0:
                    dx = value[spare : spare + 1] + value[spare + 2 : spare + 3] - x_own[:, lanes]
                    dy = value[spare + 1 : spare + 2] + value[spare + 3 : spare + 4] - y_own[:, lanes]
                    w = scale[:, lanes] * jnp.maximum(-(cosine * dx + sine * dy), 0.0)
                    weights[k, :, lanes] = w
                else:
                    w = weights[k, :, lanes]
                term = all_rows(w) * value
                total = term if total is None else total + term
            share = divisor(lanes, columns[c])
            value = (base[c, :, lanes] + columns[c] * total) * share
            shares[c, :, lanes] = share
            hi, lo = split2(value)
            lhs[c, 0:rows, lanes] = hi
            lhs[c, rows : 2 * rows, lanes] = lo
        pack(chunks + c, c)
        send(chunks + c)
        own(chunks + c)

    for side in range(2):
        lanes = slice(side * half, (side + 1) * half)
        for k in range(slots):
            every = lhs[...].reshape(chunks * 2 * rows, nodes)
            both = jnp.dot(every, hot[k, 0:nodes, lanes], preferred_element_type=f32)
            w = all_rows(weights[k, :, lanes])
            for c in range(chunks):
                at = c * 2 * rows
                term = w * (both[at : at + rows] + both[at + rows : at + 2 * rows])
                if k == 0:
                    acc[c, :, lanes] = term
                elif k < slots - 1:
                    acc[c, :, lanes] += term
                else:
                    share = shares[c, :, lanes]
                    total = acc[c, :, lanes] + term
                    acc[c, :, lanes] = (base[c, :, lanes] + columns[c] * total) * share
                    shares[c, :, lanes] = columns[c] * share

    def result_of(c):
        band_of = pl.ds(c * PER, PER)
        return pltpu.make_async_copy(out_ref.at[band_of], out_hbm.at[band_of], out_sem.at[c])

    for c in range(chunks):
        arrive(chunks + c)
        far = ghosts_of(chunks + c)
        for side in range(2):
            lanes = slice(side * half, (side + 1) * half)
            total = None
            for k in range(slots):
                term = all_rows(weights[k, :, lanes]) * product(
                    far, k, nodes, nodes + ghosts, side
                )
                total = term if total is None else total + term
            value = acc[c, :, lanes] + shares[c, :, lanes] * total
            for j in range(PER):
                out_ref[c * PER + j, 0:main, lanes] = value[j * main : (j + 1) * main]
                at = tail + j * rest
                out_ref[c * PER + j, main:dirs, lanes] = value[at : at + rest]
        result_of(c).start()

    for c in range(chunks):
        result_of(c).wait()
    for stage in range(2 * chunks):
        for off in range(1, n_mesh):
            to = lax.rem(me + off, n_mesh)
            copy_of(stage, off, to, me, to).wait_send()

    @pl.when(fi < n_freq - 1)
    def _():
        up_copy.wait_send()

    @pl.when(fi > 0)
    def _():
        down_copy.wait_send()


def hand_over(swept, result, sem):
    band = swept.shape[0]
    copies = [
        pltpu.make_async_copy(swept.at[j], result.at[j], sem.at[j]) for j in range(band)
    ]
    for copy in copies:
        copy.start()
    for copy in copies:
        copy.wait()


def local(n_mesh, n_freq, spectra, coords, inv_area, wind_vector, neighbours, send_nodes, send_count):
    band, dirs, nodes = spectra.shape
    cap = send_nodes.shape[1]
    slots = neighbours.shape[0]
    ghosts = n_mesh * cap
    chunks = band // PER
    main = dirs // 8 * 8
    rows = PER * main + -(-(PER * (dirs - main) + 4) // 8) * 8
    f32, bf16, i32 = jnp.float32, jnp.bfloat16, jnp.int32
    hbm = pl.BlockSpec(memory_space=pltpu.HBM)
    swept = pl.pallas_call(
        functools.partial(kernel, n_mesh, n_freq, dirs, cap),
        out_shape=jax.ShapeDtypeStruct(spectra.shape, f32),
        in_specs=[hbm] * 7,
        out_specs=hbm,
        scratch_shapes=[
            pltpu.VMEM(spectra.shape, f32),
            pltpu.VMEM(spectra.shape, f32),
            pltpu.VMEM(coords.shape, f32),
            pltpu.VMEM((1, nodes), f32),
            pltpu.VMEM(wind_vector.shape, f32),
            pltpu.VMEM(neighbours.shape, i32),
            pltpu.VMEM(send_nodes.shape, i32),
            pltpu.SMEM(send_count.shape, i32),
            pltpu.VMEM((chunks, 2 * rows, nodes), bf16),
            pltpu.VMEM((slots, chunks, rows, nodes), f32),
            pltpu.VMEM((chunks, rows, nodes), f32),
            pltpu.VMEM((chunks, rows, nodes), f32),
            pltpu.VMEM((chunks, rows, nodes), f32),
            pltpu.VMEM((slots, main + rows - PER * main, nodes), f32),
            pltpu.VMEM((slots, nodes + ghosts, nodes), bf16),
            pltpu.VMEM((nodes, ghosts), bf16),
            pltpu.VMEM((2 * chunks, n_mesh, rows * cap // LANES, LANES), f32),
            pltpu.VMEM((2 * chunks, n_mesh, rows * cap // LANES, LANES), f32),
            pltpu.VMEM((REACH, dirs, nodes), f32),
            pltpu.VMEM((UP_REACH, dirs, nodes), f32),
            pltpu.SemaphoreType.DMA((7,)),
            pltpu.SemaphoreType.DMA((2 * chunks, n_mesh)),
            pltpu.SemaphoreType.DMA((2 * chunks, n_mesh)),
            pltpu.SemaphoreType.DMA((4,)),
            pltpu.SemaphoreType.DMA((chunks,)),
        ],
        compiler_params=pltpu.CompilerParams(
            collective_id=0, has_side_effects=True, vmem_limit_bytes=64 * 1024 * 1024
        ),
        cost_estimate=pl.CostEstimate(
            flops=4 * 2 * band * dirs * (nodes + ghosts) * nodes * slots,
            bytes_accessed=2 * 4 * band * dirs * nodes,
            transcendentals=0,
        ),
    )(spectra, coords, inv_area.reshape(1, nodes), wind_vector, neighbours, send_nodes, send_count)
    return pl.pallas_call(
        hand_over,
        out_shape=jax.ShapeDtypeStruct(spectra.shape, f32),
        in_specs=[hbm],
        out_specs=hbm,
        scratch_shapes=[pltpu.SemaphoreType.DMA((band,))],
        compiler_params=pltpu.CompilerParams(vmem_limit_bytes=64 * 1024 * 1024),
    )(swept)


def solution(mesh):
    in_specs = (
        P("freq", None, "mesh"),
        P(None, "mesh"),
        P("mesh"),
        P(None, "mesh"),
        P(None, "mesh"),
        P("mesh", None),
        P("mesh"),
    )
    return jax.shard_map(
        functools.partial(local, mesh.shape["mesh"], mesh.shape["freq"]),
        mesh=mesh, in_specs=in_specs, out_specs=P("freq", None, "mesh"), check_vma=False,
    )
```

```python
import functools
import math

import jax
import jax.numpy as jnp
from jax import lax
from jax.experimental import pallas as pl
from jax.experimental.pallas import tpu as pltpu
from jax.sharding import PartitionSpec as P

NF = 36
REACH = 3
UP_REACH = REACH - 1
UP_SHIFT = 1
DOWN_SHIFT = 3

time_step = 0.5
group_scale = 0.8
quad_coupling = 0.25
wind_growth = 0.1
freq_ratio = 1.1

MESH = pl.DeviceIdType.MESH
PER = 3
LANES = 128


def split2(x):
    hi = x.astype(jnp.bfloat16)
    lo = (x - hi.astype(jnp.float32)).astype(jnp.bfloat16)
    return hi, lo


def roll_rows(x, shift):
    count = x.shape[0]
    cut = (-shift) % count
    return jnp.concatenate([x[cut:], x[:cut]], axis=0)


def kernel(
    n_mesh, n_freq, dirs, cap,
    spec_hbm, coords_hbm, inv_hbm, wind_hbm, nb_hbm, send_hbm, count_hbm,
    out_hbm,
    out_ref, spec_ref, coords_ref, inv_ref, wind_ref, nb_ref, send_ref, count_ref,
    lhs, picked, base, acc, shares, weights, hot, hot_send, pay, recv, halo_lo, halo_hi,
    in_sem, send_sem, recv_sem, halo_sem, out_sem,
):
    band = spec_ref.shape[0]
    nodes = spec_ref.shape[2]
    slots = nb_ref.shape[0]
    ghosts = n_mesh * cap
    chunks = band // PER
    main = dirs // 8 * 8
    rest = dirs - main
    rows = lhs.shape[1] // 2
    tail = PER * main
    spare = tail + PER * rest
    tail_rows = rows - tail
    half = nodes // 2
    groups = LANES // cap
    depth = rows // groups
    f32 = jnp.float32
    bf16 = jnp.bfloat16
    me = lax.axis_index("mesh")
    fi = lax.axis_index("freq")

    pairs = (
        (send_hbm, send_ref), (count_hbm, count_ref), (spec_hbm, spec_ref),
        (coords_hbm, coords_ref), (nb_hbm, nb_ref), (inv_hbm, inv_ref), (wind_hbm, wind_ref),
    )
    loads = [pltpu.make_async_copy(a, b, in_sem.at[i]) for i, (a, b) in enumerate(pairs)]
    for load in loads:
        load.start()

    barrier = pltpu.get_barrier_semaphore()
    for off in range(1, n_mesh):
        pl.semaphore_signal(
            barrier, inc=1, device_id={"mesh": lax.rem(me + off, n_mesh)}, device_id_type=MESH
        )

    @pl.when(fi > 0)
    def _():
        pl.semaphore_signal(barrier, inc=1, device_id={"freq": fi - 1}, device_id_type=MESH)

    @pl.when(fi < n_freq - 1)
    def _():
        pl.semaphore_signal(barrier, inc=1, device_id={"freq": fi + 1}, device_id_type=MESH)

    row_id = lax.broadcasted_iota(jnp.int32, (main + tail_rows, LANES), 0)
    direction = jnp.where(row_id < main, row_id, main + (row_id - main) % rest)
    angle = (direction.astype(f32) + 0.5) * (2.0 * math.pi / dirs)
    real = row_id < main + PER * rest
    cosine = jnp.where(real, jnp.cos(angle), 0.0)[:, 0:1]
    sine = jnp.where(real, jnp.sin(angle), 0.0)[:, 0:1]
    ratios = []
    for j in range(band):
        value = jnp.float32(freq_ratio ** (j - NF // 2))
        for b in range(1, n_freq):
            value = jnp.where(fi == b, jnp.float32(freq_ratio ** (b * band + j - NF // 2)), value)
        ratios.append(value)
    speeds = [group_scale / r for r in ratios]

    loads[0].wait()
    send_row = jnp.concatenate([send_ref[d : d + 1, :] for d in range(n_mesh)], axis=1)
    lane = lax.broadcasted_iota(jnp.int32, (1, ghosts), 1)
    limit = jnp.zeros((1, ghosts), jnp.int32)
    loads[1].wait()
    for d in range(n_mesh):
        limit = jnp.where(lane // cap == d, count_ref[d], limit)
    send_row = jnp.where(lane % cap < limit, send_row, -1)
    hot_send[...] = (
        (lax.broadcasted_iota(jnp.int32, (nodes, ghosts), 0) == send_row).astype(f32).astype(bf16)
    )

    def copy_of(stage, off, src_rank, dst_rank, target):
        return pltpu.make_async_remote_copy(
            src_ref=pay.at[stage, src_rank],
            dst_ref=recv.at[stage, dst_rank],
            send_sem=send_sem.at[stage, off],
            recv_sem=recv_sem.at[stage, off],
            device_id={"mesh": target},
            device_id_type=MESH,
        )

    def pack(stage, c):
        both = jnp.dot(lhs[c], hot_send[...], preferred_element_type=f32)
        value = both[:rows] + both[rows:]
        bands = [value[g * depth : (g + 1) * depth] for g in range(groups)]
        for d in range(n_mesh):
            pay[stage, d] = jnp.concatenate(
                [part[:, d * cap : (d + 1) * cap] for part in bands], axis=1
            )

    def send(stage):
        for off in range(1, n_mesh):
            to = lax.rem(me + off, n_mesh)
            copy_of(stage, off, to, me, to).start()

    def own(stage):
        recv[stage, me] = pay[stage, me]

    def leave(stage):
        for off in range(1, n_mesh):
            to = lax.rem(me + off, n_mesh)
            copy_of(stage, off, to, me, to).wait_send()

    def arrive(stage):
        for off in range(1, n_mesh):
            copy_of(stage, off, 0, me, lax.rem(me + off, n_mesh)).wait_recv()

    def ghosts_of(stage):
        blocks = [recv[stage, d] for d in range(n_mesh)]
        bands = [
            jnp.concatenate([block[:, g * cap : (g + 1) * cap] for block in blocks], axis=1)
            for g in range(groups)
        ]
        hi, lo = split2(jnp.concatenate(bands, axis=0))
        return jnp.concatenate([hi, lo], axis=0)

    def split_chunk(c, value):
        hi, lo = split2(value)
        lhs[c, 0:rows] = hi
        lhs[c, rows : 2 * rows] = lo

    loads[2].wait()
    loads[3].wait()
    x_own = coords_ref[0:1, :]
    y_own = coords_ref[1:2, :]
    remains = []
    for row in (x_own, y_own):
        hi, lo = split2(row)
        remains.append((row - hi.astype(f32)) - lo.astype(f32))
    for c in range(chunks):
        parts = [spec_ref[c * PER + j, 0:main, :] for j in range(PER)]
        parts += [spec_ref[c * PER + j, main:dirs, :] for j in range(PER)]
        if c == 0:
            parts += [x_own, y_own] + remains
        else:
            parts += [jnp.zeros((rows - spare, nodes), f32)]
        split_chunk(c, jnp.concatenate(parts, axis=0))
        pack(c, c)
        if c == 0:
            expected = (n_mesh - 1) + (fi > 0).astype(jnp.int32)
            expected = expected + (fi < n_freq - 1).astype(jnp.int32)
            pl.semaphore_wait(barrier, expected)
        if c < chunks - 1:
            send(c)

    up_copy = pltpu.make_async_remote_copy(
        src_ref=spec_ref.at[pl.ds(band - REACH, REACH)], dst_ref=halo_lo,
        send_sem=halo_sem.at[0], recv_sem=halo_sem.at[1],
        device_id={"freq": lax.rem(fi + 1, n_freq)}, device_id_type=MESH,
    )
    down_copy = pltpu.make_async_remote_copy(
        src_ref=spec_ref.at[pl.ds(0, UP_REACH)], dst_ref=halo_hi,
        send_sem=halo_sem.at[2], recv_sem=halo_sem.at[3],
        device_id={"freq": lax.rem(fi + n_freq - 1, n_freq)}, device_id_type=MESH,
    )

    @pl.when(fi < n_freq - 1)
    def _():
        up_copy.start()

    @pl.when(fi > 0)
    def _():
        down_copy.start()

    @pl.when(fi == 0)
    def _():
        halo_lo[...] = jnp.zeros(halo_lo.shape, f32)

    @pl.when(fi == n_freq - 1)
    def _():
        halo_hi[...] = jnp.zeros(halo_hi.shape, f32)

    for load in loads[4:]:
        load.wait()
    for c in range(chunks):
        own(c)

    def product(part, k, first, last, side):
        both = jnp.dot(
            part, hot[k, first:last, side * half : (side + 1) * half], preferred_element_type=f32
        )
        return both[:rows] + both[rows:]

    along = cosine[:main] * wind_ref[0:1, :] + sine[:main] * wind_ref[1:2, :]
    along_rest = (
        cosine[main : main + rest] * wind_ref[0:1, :] + sine[main : main + rest] * wind_ref[1:2, :]
    )
    along = jnp.concatenate([along, along_rest], axis=0)

    def sources(j):
        own_bin = spec_ref[j]
        upper = spec_ref[j + UP_REACH] if j + UP_REACH < band else halo_hi[j + UP_REACH - band]
        lower = spec_ref[j - REACH] if j >= REACH else halo_lo[j]
        p1 = roll_rows(upper, -UP_SHIFT)
        m1 = roll_rows(lower, DOWN_SHIFT)
        p2 = roll_rows(upper, UP_SHIFT)
        m2 = roll_rows(lower, -DOWN_SHIFT)
        quad = quad_coupling * (
            own_bin * own_bin * (p1 + m1 + p2 + m2) - 2.0 * own_bin * (p1 * m1 + p2 * m2)
        )
        growth = wind_growth * jnp.maximum(along * ratios[j] - 1.0, 0.0)
        value = own_bin + time_step * (quad + growth * own_bin)
        c, at = divmod(j, PER)
        base[c, at * main : (at + 1) * main, :] = value[:main]
        base[c, tail + at * rest : tail + (at + 1) * rest, :] = value[main:]

    for c in range(chunks):
        base[c, spare:rows, :] = jnp.zeros((rows - spare, nodes), f32)

    def hot_columns(k):
        entry = nb_ref[k : k + 1, :]
        ids = lax.broadcasted_iota(jnp.int32, (nodes + ghosts, nodes), 0)
        hot[k] = (ids == entry).astype(f32).astype(bf16)

    def pick_local(k):
        every = lhs[...].reshape(chunks * 2 * rows, nodes)
        for side in range(2):
            lanes = slice(side * half, (side + 1) * half)
            both = jnp.dot(every, hot[k, 0:nodes, lanes], preferred_element_type=f32)
            for c in range(chunks):
                at = c * 2 * rows
                picked[k, c, :, lanes] = both[at : at + rows] + both[at + rows : at + 2 * rows]

    middle = list(range(REACH, band - UP_REACH))
    outer = [j for j in range(band) if j not in middle]
    first = slots // 2
    hot_columns(0)
    for k in range(slots):
        if k == first:
            @pl.when(fi > 0)
            def _():
                up_copy.wait_recv()

            @pl.when(fi < n_freq - 1)
            def _():
                down_copy.wait_recv()

        if k == slots - 2:
            leave(0)
            send(chunks - 1)
        if k + 1 < slots:
            hot_columns(k + 1)
        pick_local(k)
        if k < first:
            for j in middle[k::first]:
                sources(j)
        else:
            for j in outer[k - first :: slots - first]:
                sources(j)

    scale = time_step * inv_ref[...]
    chunk_row = lax.broadcasted_iota(jnp.int32, (rows, LANES), 0)

    def speed_column(c):
        column = jnp.zeros((rows, LANES), f32)
        for j in range(PER):
            inside = (chunk_row >= j * main) & (chunk_row < (j + 1) * main)
            behind = (chunk_row >= tail + j * rest) & (chunk_row < tail + (j + 1) * rest)
            column = jnp.where(inside | behind, speeds[c * PER + j], column)
        return column[:, 0:1]

    def all_rows(w):
        return jnp.concatenate([w[:main]] * PER + [w[main:]], axis=0)

    def divisor(lanes, column):
        wsum = weights[0, :, lanes]
        for k in range(1, slots):
            wsum = wsum + weights[k, :, lanes]
        return 1.0 / (1.0 + column * all_rows(wsum))

    columns = [speed_column(c) for c in range(chunks)]
    for c in range(chunks):
        arrive(c)
        far = ghosts_of(c)
        for side in range(2):
            lanes = slice(side * half, (side + 1) * half)
            total = None
            for k in range(slots):
                value = picked[k, c, :, lanes] + product(far, k, nodes, nodes + ghosts, side)
                if c == 0:
                    dx = value[spare : spare + 1] + value[spare + 2 : spare + 3] - x_own[:, lanes]
                    dy = value[spare + 1 : spare + 2] + value[spare + 3 : spare + 4] - y_own[:, lanes]
                    w = scale[:, lanes] * jnp.maximum(-(cosine * dx + sine * dy), 0.0)
                    weights[k, :, lanes] = w
                else:
                    w = weights[k, :, lanes]
                term = all_rows(w) * value
                total = term if total is None else total + term
            share = divisor(lanes, columns[c])
            value = (base[c, :, lanes] + columns[c] * total) * share
            shares[c, :, lanes] = share
            hi, lo = split2(value)
            lhs[c, 0:rows, lanes] = hi
            lhs[c, rows : 2 * rows, lanes] = lo
        pack(chunks + c, c)
        send(chunks + c)
        own(chunks + c)

    for side in range(2):
        lanes = slice(side * half, (side + 1) * half)
        for k in range(slots):
            every = lhs[...].reshape(chunks * 2 * rows, nodes)
            both = jnp.dot(every, hot[k, 0:nodes, lanes], preferred_element_type=f32)
            w = all_rows(weights[k, :, lanes])
            for c in range(chunks):
                at = c * 2 * rows
                term = w * (both[at : at + rows] + both[at + rows : at + 2 * rows])
                if k == 0:
                    acc[c, :, lanes] = term
                elif k < slots - 1:
                    acc[c, :, lanes] += term
                else:
                    share = shares[c, :, lanes]
                    total = acc[c, :, lanes] + term
                    acc[c, :, lanes] = (base[c, :, lanes] + columns[c] * total) * share
                    shares[c, :, lanes] = columns[c] * share

    def result_of(c):
        band_of = pl.ds(c * PER, PER)
        return pltpu.make_async_copy(out_ref.at[band_of], out_hbm.at[band_of], out_sem.at[c])

    for c in range(chunks):
        arrive(chunks + c)
        far = ghosts_of(chunks + c)
        for side in range(2):
            lanes = slice(side * half, (side + 1) * half)
            total = None
            for k in range(slots):
                term = all_rows(weights[k, :, lanes]) * product(
                    far, k, nodes, nodes + ghosts, side
                )
                total = term if total is None else total + term
            value = acc[c, :, lanes] + shares[c, :, lanes] * total
            for j in range(PER):
                out_ref[c * PER + j, 0:main, lanes] = value[j * main : (j + 1) * main]
                at = tail + j * rest
                out_ref[c * PER + j, main:dirs, lanes] = value[at : at + rest]
        result_of(c).start()

    for c in range(chunks):
        result_of(c).wait()
    for stage in range(1, 2 * chunks):
        leave(stage)

    @pl.when(fi < n_freq - 1)
    def _():
        up_copy.wait_send()

    @pl.when(fi > 0)
    def _():
        down_copy.wait_send()


def hand_over(swept, result, held, in_sem, out_sem):
    parts = [pl.ds(j, PER) for j in range(0, swept.shape[0], PER)]
    loads = [
        pltpu.make_async_copy(swept.at[p], held.at[p], in_sem.at[i]) for i, p in enumerate(parts)
    ]
    stores = [
        pltpu.make_async_copy(held.at[p], result.at[p], out_sem.at[i]) for i, p in enumerate(parts)
    ]
    for load in loads:
        load.start()
    for load, store in zip(loads, stores):
        load.wait()
        store.start()
    for store in stores:
        store.wait()


def local(n_mesh, n_freq, spectra, coords, inv_area, wind_vector, neighbours, send_nodes, send_count):
    band, dirs, nodes = spectra.shape
    cap = send_nodes.shape[1]
    slots = neighbours.shape[0]
    ghosts = n_mesh * cap
    chunks = band // PER
    main = dirs // 8 * 8
    rows = PER * main + -(-(PER * (dirs - main) + 4) // 8) * 8
    f32, bf16, i32 = jnp.float32, jnp.bfloat16, jnp.int32
    hbm = pl.BlockSpec(memory_space=pltpu.HBM)
    swept = pl.pallas_call(
        functools.partial(kernel, n_mesh, n_freq, dirs, cap),
        out_shape=jax.ShapeDtypeStruct(spectra.shape, f32),
        in_specs=[hbm] * 7,
        out_specs=hbm,
        scratch_shapes=[
            pltpu.VMEM(spectra.shape, f32),
            pltpu.VMEM(spectra.shape, f32),
            pltpu.VMEM(coords.shape, f32),
            pltpu.VMEM((1, nodes), f32),
            pltpu.VMEM(wind_vector.shape, f32),
            pltpu.VMEM(neighbours.shape, i32),
            pltpu.VMEM(send_nodes.shape, i32),
            pltpu.SMEM(send_count.shape, i32),
            pltpu.VMEM((chunks, 2 * rows, nodes), bf16),
            pltpu.VMEM((slots, chunks, rows, nodes), f32),
            pltpu.VMEM((chunks, rows, nodes), f32),
            pltpu.VMEM((chunks, rows, nodes), f32),
            pltpu.VMEM((chunks, rows, nodes), f32),
            pltpu.VMEM((slots, main + rows - PER * main, nodes), f32),
            pltpu.VMEM((slots, nodes + ghosts, nodes), bf16),
            pltpu.VMEM((nodes, ghosts), bf16),
            pltpu.VMEM((2 * chunks, n_mesh, rows * cap // LANES, LANES), f32),
            pltpu.VMEM((2 * chunks, n_mesh, rows * cap // LANES, LANES), f32),
            pltpu.VMEM((REACH, dirs, nodes), f32),
            pltpu.VMEM((UP_REACH, dirs, nodes), f32),
            pltpu.SemaphoreType.DMA((7,)),
            pltpu.SemaphoreType.DMA((2 * chunks, n_mesh)),
            pltpu.SemaphoreType.DMA((2 * chunks, n_mesh)),
            pltpu.SemaphoreType.DMA((4,)),
            pltpu.SemaphoreType.DMA((chunks,)),
        ],
        compiler_params=pltpu.CompilerParams(
            collective_id=0, has_side_effects=True, vmem_limit_bytes=64 * 1024 * 1024
        ),
        cost_estimate=pl.CostEstimate(
            flops=4 * 2 * band * dirs * (nodes + ghosts) * nodes * slots,
            bytes_accessed=2 * 4 * band * dirs * nodes,
            transcendentals=0,
        ),
    )(spectra, coords, inv_area.reshape(1, nodes), wind_vector, neighbours, send_nodes, send_count)
    return pl.pallas_call(
        hand_over,
        out_shape=jax.ShapeDtypeStruct(spectra.shape, f32),
        in_specs=[hbm],
        out_specs=hbm,
        scratch_shapes=[
            pltpu.VMEM(spectra.shape, f32),
            pltpu.SemaphoreType.DMA((chunks,)),
            pltpu.SemaphoreType.DMA((chunks,)),
        ],
        compiler_params=pltpu.CompilerParams(vmem_limit_bytes=64 * 1024 * 1024),
    )(swept)


def solution(mesh):
    in_specs = (
        P("freq", None, "mesh"),
        P(None, "mesh"),
        P("mesh"),
        P(None, "mesh"),
        P(None, "mesh"),
        P("mesh", None),
        P("mesh"),
    )
    return jax.shard_map(
        functools.partial(local, mesh.shape["mesh"], mesh.shape["freq"]),
        mesh=mesh, in_specs=in_specs, out_specs=P("freq", None, "mesh"), check_vma=False,
    )
```
